32 devices in a mesh: rows: 8 (over z, x), heads: 4 (over y, core).
Axes of the slice: x: 2, y: 2, z: 4, core: 2. Of those that a mesh axis runs over, the one named last changes fastest.
Arguments:
- latents: bfloat16 [8, 16, 32, 1280], P('rows', None, None, 'heads'), may hold values from -6 to 6
- text: bfloat16 [4, 77, 2048], replicated, may hold values from -6 to 6
- step_count: int32 [4], replicated, may hold values from 1 to 4, as said below
- time_index: int32 [4], replicated, may hold values from 0 to 3, as said below
- conv1_w: bfloat16 [3, 3, 1280, 1280], P(None, None, 'rows', 'heads'), may hold values from -0.0546875 to 0.0546875
- conv2_w: bfloat16 [3, 3, 1280, 1280], P(None, None, 'rows', 'heads'), may hold values from -0.0546875 to 0.0546875
- time_w: bfloat16 [1280, 1280], P('rows', 'heads'), may hold values from -0.15625 to 0.15625
- proj_in_w: bfloat16 [1280, 1280], P('rows', 'heads'), may hold values from -0.15625 to 0.15625
- qkv_w: bfloat16 [1280, 3, 1280], P('rows', None, 'heads'), may hold values from -0.15625 to 0.15625
- self_out_w: bfloat16 [1280, 1280], P('heads', 'rows'), may hold values from -1.25 to 1.25
- cross_q_w: bfloat16 [1280, 1280], P('rows', 'heads'), may hold values from -0.15625 to 0.15625
- cross_kv_w: bfloat16 [2048, 2, 1280], P('rows', None, 'heads'), may hold values from -0.125 to 0.125
- cross_out_w: bfloat16 [1280, 1280], P('heads', 'rows'), may hold values from -0.625 to 0.625
- ff_in_w: bfloat16 [1280, 2, 5120], P('rows', None, 'heads'), may hold values from -0.15625 to 0.15625
- ff_out_w: bfloat16 [5120, 1280], P('heads', 'rows'), may hold values from -0.078125 to 0.078125
- proj_out_w: bfloat16 [1280, 1280], P('rows', 'heads'), may hold values from -0.15625 to 0.15625
- gn_params: float32 [3, 2, 1280], P(None, None, 'heads'), may hold values from -1 to 1.5, as said below
- ln_params: float32 [3, 2, 1280], P(None, None, 'heads'), may hold values from -1 to 1.5, as said below
- biases: float32 [8, 1280], P(None, 'heads'), may hold values from -1.5 to 1.5
- ff_bias: float32 [2, 5120], P(None, 'heads'), may hold values from -1.5 to 1.5
- cotangent: bfloat16 [8, 16, 32, 1280], P('rows', None, None, 'heads'), may hold values from -6 to 6
Outputs:
- output: bfloat16 [8, 16, 32, 1280], P('rows', None, None, 'heads')
- latents_grad: float32 [8, 16, 32, 1280], P('rows', None, None, 'heads')
- conv1_w_grad: float32 [3, 3, 1280, 1280], P(None, None, 'rows', 'heads')
- conv2_w_grad: float32 [3, 3, 1280, 1280], P(None, None, 'rows', 'heads')
- time_w_grad: float32 [1280, 1280], P('rows', 'heads')
- proj_in_w_grad: float32 [1280, 1280], P('rows', 'heads')
- qkv_w_grad: float32 [1280, 3, 1280], P('rows', None, 'heads')
- self_out_w_grad: float32 [1280, 1280], P('heads', 'rows')
- cross_q_w_grad: float32 [1280, 1280], P('rows', 'heads')
- cross_kv_w_grad: float32 [2048, 2, 1280], P('rows', None, 'heads')
- cross_out_w_grad: float32 [1280, 1280], P('heads', 'rows')
- ff_in_w_grad: float32 [1280, 2, 5120], P('rows', None, 'heads')
- ff_out_w_grad: float32 [5120, 1280], P('heads', 'rows')
- proj_out_w_grad: float32 [1280, 1280], P('rows', 'heads')
- gn_params_grad: float32 [3, 2, 1280], P(None, None, 'heads')
- ln_params_grad: float32 [3, 2, 1280], P(None, None, 'heads')
- biases_grad: float32 [8, 1280], P(None, 'heads')
- ff_bias_grad: float32 [2, 5120], P(None, 'heads')
The draws below stay inside these ranges and needn't reach their ends.
Inputs may be any that keep to these rules, and one draw needn't show every extreme that they name: `step_count`: each image's number of student steps; some image has 4 and some image has 1. `time_index`: below the image's step_count. `gn_params`: gains (index 0 of the second dimension) lie in 0.5 to 1.5, shifts in -1 to 1. `ln_params`: gains (index 0 of the second dimension) lie in 0.5 to 1.5, shifts in -1 to 1.
All inputs are finite; a program needn't handle non-finite values.
Results may differ from the reference program's by a relative error of at most 0.025.
Values may be sent and summed in bfloat16 or wider, within the bound.
No kernel may reach another device: no remote copies, remote signals or barrier semaphores. Data moves between devices by JAX's collectives and lax.ppermute only.
A program may use at most 320 MiB of HBM per device.

```python
import math
import jax
import jax.numpy as jnp
from jax import lax

C = 1280
HEADS = 20
DH = 64
GROUPS = 32
FF = 5120
TD = 2048
TEXT = 77
HEIGHT = 32
WIDTH = 32
HALF = 16
IMAGES = 4


def student_plan(key):
    counts = jax.random.randint(jax.random.fold_in(key, 11), (IMAGES,), 1, 5)
    chosen = jax.random.randint(jax.random.fold_in(key, 12), (), 0, IMAGES)
    places = jnp.arange(IMAGES)
    counts = jnp.where(places == chosen, 4, counts)
    counts = jnp.where(places == (chosen + 1) % IMAGES, 1, counts)
    stamps = jax.random.randint(jax.random.fold_in(key, 13), (IMAGES,), 0, counts)
    stamps = jnp.where(places == chosen, 3, stamps)
    return (counts.astype(jnp.int32), stamps.astype(jnp.int32))


def norm_table(key):
    gain_part = jax.random.uniform(jax.random.fold_in(key, 1), (3, 1, C), jnp.float32, 0.5, 1.5)
    shift_part = jnp.clip(0.3 * jax.random.normal(jax.random.fold_in(key, 2), (3, 1, C), jnp.float32), -1.0, 1.0)
    return jnp.concatenate([gain_part, shift_part], axis=1)


def draw_step_count(key, part):
    counts, stamps = student_plan(key)
    return counts


def draw_time_index(key, part):
    counts, stamps = student_plan(key)
    return stamps


def draw_gn_params(key, part):
    key = jax.random.fold_in(key, 3)
    return norm_table(key)


def draw_ln_params(key, part):
    key = jax.random.fold_in(key, 5)
    return norm_table(key)


def level_of(stream_key, dims, split, least, high):
    factor_of = 1.0
    for axis_at, blocks in split:
        draws = jax.random.uniform(jax.random.fold_in(jax.random.fold_in(stream_key, 6), axis_at), (blocks,), jnp.float32, least / len(split), high / len(split))
        factor_of = factor_of * jnp.repeat(jnp.exp(draws), dims[axis_at] // blocks).reshape((-1,) + (1,) * (len(dims) - 1 - axis_at))
    return factor_of


def normal_values(own_key, extent, scale, reach, shards=(), kind=jnp.bfloat16):
    array = jax.random.normal(own_key, extent, jnp.float32) * scale
    if len(shards) > 0:
        array = level_of(own_key, extent, shards, -0.22, 0.18) * array
    return jnp.clip(array, min=-reach, max=reach).astype(kind)


def setup_inputs(seed: int = 0) -> dict:
    seeds = jax.random.split(jax.random.key(seed), 22)
    return {
        "latents": normal_values(seeds[0], (2 * IMAGES, HALF, WIDTH, C), 1.0, 6.0, ((0, 8), (3, 4))),
        "text": normal_values(seeds[1], (IMAGES, TEXT, TD), 1.0, 6.0),
        "step_count": draw_step_count(jax.random.fold_in(seeds[21], 71), 0),
        "time_index": draw_time_index(jax.random.fold_in(seeds[21], 71), 0),
        "conv1_w": normal_values(seeds[4], (3, 3, C, C), (9 * C) ** -0.5, 0.0546875, ((2, 8), (3, 4))),
        "conv2_w": normal_values(seeds[5], (3, 3, C, C), (9 * C) ** -0.5, 0.0546875, ((2, 8), (3, 4))),
        "time_w": normal_values(seeds[6], (C, C), C ** -0.5, 0.15625, ((0, 8), (1, 4))),
        "proj_in_w": normal_values(seeds[7], (C, C), C ** -0.5, 0.15625, ((0, 8), (1, 4))),
        "qkv_w": normal_values(seeds[8], (C, 3, C), C ** -0.5, 0.15625, ((0, 8), (2, 4))),
        "self_out_w": normal_values(seeds[9], (C, C), (max(C // 64, 4)) ** -0.5, 1.25, ((0, 4), (1, 8))),
        "cross_q_w": normal_values(seeds[10], (C, C), C ** -0.5, 0.15625, ((0, 8), (1, 4))),
        "cross_kv_w": normal_values(seeds[11], (TD, 2, C), TD ** -0.5, 0.125, ((0, 8), (2, 4))),
        "cross_out_w": normal_values(seeds[12], (C, C), (max(C // 16, 4)) ** -0.5, 0.625, ((0, 4), (1, 8))),
        "ff_in_w": normal_values(seeds[13], (C, 2, FF), C ** -0.5, 0.15625, ((0, 8), (2, 4))),
        "ff_out_w": normal_values(seeds[14], (FF, C), FF ** -0.5, 0.078125, ((0, 4), (1, 8))),
        "proj_out_w": normal_values(seeds[15], (C, C), C ** -0.5, 0.15625, ((0, 8), (1, 4))),
        "gn_params": draw_gn_params(jax.random.fold_in(seeds[21], 71), 0),
        "ln_params": draw_ln_params(jax.random.fold_in(seeds[21], 71), 0),
        "biases": normal_values(seeds[18], (8, C), 0.3, 1.5, ((1, 4),), jnp.float32),
        "ff_bias": normal_values(seeds[19], (2, FF), 0.3, 1.5, ((1, 4),), jnp.float32),
        "cotangent": normal_values(seeds[20], (2 * IMAGES, HALF, WIDTH, C), 1.0, 6.0, ((0, 8), (3, 4))),
    }


@jax.custom_vjp
def low(v):
    return lax.optimization_barrier(v.astype(jnp.bfloat16)).astype(jnp.float32)

@jax.custom_vjp
def low_back(v):
    return v

def low_keep(v):
    return (low(v), None)

def low_pass(kept, grad):
    return (grad,)

def back_keep(v):
    return (v, None)

def back_low(kept, grad):
    return (low(grad),)
low.defvjp(low_keep, low_pass)
low_back.defvjp(back_keep, back_low)
HIGH = lax.Precision.HIGHEST

def both_round(tensor):
    return low(low_back(tensor))

def group_norm(field, params, epsilon):
    count_b = field.shape[0]
    grouped = field.reshape(count_b, HEIGHT * WIDTH, GROUPS, C // GROUPS)
    center = lax.optimization_barrier(jnp.mean(grouped, axis=(1, 3), keepdims=True))
    spread = lax.optimization_barrier(jnp.mean(jnp.square(grouped - center), axis=(1, 3), keepdims=True))
    normed = ((grouped - center) * lax.rsqrt(spread + epsilon)).reshape(field.shape)
    return normed * params[0] + params[1]

def layer_norm(field, params):
    center = lax.optimization_barrier(jnp.mean(field, axis=-1, keepdims=True))
    spread = lax.optimization_barrier(jnp.mean(jnp.square(field - center), axis=-1, keepdims=True))
    return (field - center) * lax.rsqrt(spread + 1e-05) * params[0] + params[1]

def convolve(field, kernel):
    return lax.conv_general_dilated(field, kernel, (1, 1), 'SAME', dimension_numbers=('NHWC', 'HWIO', 'NHWC'), precision=HIGH)

def attend_image(packed):
    queries, key_rows, value_rows = packed
    q_heads = queries.reshape(queries.shape[0], HEADS, DH)
    k_heads = key_rows.reshape(key_rows.shape[0], HEADS, DH)
    v_heads = value_rows.reshape(value_rows.shape[0], HEADS, DH)
    scores = low_back(jnp.einsum('qhd,khd->hqk', q_heads, k_heads, precision=HIGH) * (1.0 / math.sqrt(DH)))
    probs = jax.nn.softmax(scores, axis=-1)
    joined = jnp.einsum('hqk,khd->qhd', low(probs), v_heads, precision=HIGH)
    return joined.reshape(queries.shape[0], C)

def forward(images, weights, embedding, prompts):
    conv1_w, conv2_w, time_w, proj_in_w, qkv_w, self_out_w, cross_q_w, cross_kv_w, cross_out_w, ff_in_w, ff_out_w, proj_out_w, gn_params, ln_params, biases, ff_bias = weights
    count_b = images.shape[0]
    tokens = HEIGHT * WIDTH
    act_one = low(jax.nn.silu(group_norm(images, gn_params[0], 1e-05)))
    conv_one = low_back(convolve(act_one, conv1_w) + biases[0])
    shift_time = jnp.dot(low(jax.nn.silu(embedding)), time_w, precision=HIGH) + biases[1]
    hidden_two = conv_one + shift_time[:, None, None, :]
    act_two = low(jax.nn.silu(group_norm(hidden_two, gn_params[1], 1e-05)))
    conv_two = low_back(convolve(act_two, conv2_w) + biases[2])
    resid = images + conv_two
    gin = low(group_norm(resid, gn_params[2], 1e-06)).reshape(count_b, tokens, C)
    stream = low_back(jnp.einsum('btc,cd->btd', gin, proj_in_w, precision=HIGH) + biases[3])
    n_one = low(layer_norm(stream, ln_params[0]))
    qkv = both_round(jnp.einsum('btc,cjd->btjd', n_one, qkv_w, precision=HIGH))
    attended = both_round(lax.map(jax.checkpoint(attend_image), (qkv[:, :, 0], qkv[:, :, 1], qkv[:, :, 2])))
    stream = stream + low_back(jnp.einsum('btc,cd->btd', attended, self_out_w, precision=HIGH) + biases[4])
    n_two = low(layer_norm(stream, ln_params[1]))
    cross_query = both_round(jnp.einsum('btc,cd->btd', n_two, cross_q_w, precision=HIGH))
    cross_kv = both_round(jnp.einsum('bsc,cjd->bsjd', prompts, cross_kv_w, precision=HIGH))
    cross_att = both_round(lax.map(jax.checkpoint(attend_image), (cross_query, cross_kv[:, :, 0], cross_kv[:, :, 1])))
    stream = stream + low_back(jnp.einsum('btc,cd->btd', cross_att, cross_out_w, precision=HIGH) + biases[5])
    n_three = low(layer_norm(stream, ln_params[2]))
    gate_up = low_back(jnp.einsum('btc,cjf->btjf', n_three, ff_in_w, precision=HIGH) + ff_bias)
    mixed = both_round(gate_up[:, :, 0] * jax.nn.gelu(gate_up[:, :, 1], approximate=False))
    stream = stream + low_back(jnp.einsum('btf,fd->btd', mixed, ff_out_w, precision=HIGH) + biases[6])
    projected = low_back(jnp.einsum('btc,cd->btd', low(stream), proj_out_w, precision=HIGH) + biases[7])
    return resid + projected.reshape(resid.shape)

def reference(latents, text, step_count, time_index, conv1_w, conv2_w, time_w, proj_in_w, qkv_w, self_out_w, cross_q_w, cross_kv_w, cross_out_w, ff_in_w, ff_out_w, proj_out_w, gn_params, ln_params, biases, ff_bias, cotangent):
    moment = (999 - 1000 * time_index // step_count).astype(jnp.float32)
    half_width = C // 2
    frequency = jnp.exp(-math.log(10000.0) * jnp.arange(half_width).astype(jnp.float32) / half_width)
    angles = moment[:, None] * frequency[None, :]
    embedding = jnp.concatenate([jnp.cos(angles), jnp.sin(angles)], axis=1)
    group_size = math.gcd(IMAGES, 4)
    rounds = IMAGES // group_size
    shape_in = (rounds, group_size, HEIGHT, WIDTH, C)
    params = tuple((tensor.astype(jnp.float32) for tensor in (conv1_w, conv2_w, time_w, proj_in_w, qkv_w, self_out_w, cross_q_w, cross_kv_w, cross_out_w, ff_in_w, ff_out_w, proj_out_w, gn_params, ln_params, biases, ff_bias)))

    def one_round(totals, pieces):
        images, embeds, prompts, grads_in = pieces

        def local_pass(images_in, *weights):
            return forward(images_in, weights, embeds, prompts)
        result, pull_back = jax.vjp(local_pass, images, *params)
        gradients = pull_back(grads_in)
        summed = tuple((acc_sum + new_sum for acc_sum, new_sum in zip(totals, gradients[1:])))
        return (summed, (result, gradients[0]))
    initial = tuple((jnp.zeros_like(tensor) for tensor in params))
    pieces = (latents.astype(jnp.float32).reshape(shape_in), embedding.reshape(rounds, group_size, C), text.astype(jnp.float32).reshape(rounds, group_size, TEXT, TD), cotangent.astype(jnp.float32).reshape(shape_in))
    totals, (results, latent_grads) = lax.scan(one_round, initial, pieces)
    output = results.reshape(2 * IMAGES, HALF, WIDTH, C).astype(jnp.bfloat16)
    latents_grad = latent_grads.reshape(2 * IMAGES, HALF, WIDTH, C)
    return (output, latents_grad, totals[0], totals[1], totals[2], totals[3], totals[4], totals[5], totals[6], totals[7], totals[8], totals[9], totals[10], totals[11], totals[12], totals[13], totals[14], totals[15])
```

```python
import math

import jax
import jax.numpy as jnp
from jax import lax
from jax.experimental import pallas as pl
from jax.sharding import PartitionSpec as P
from jax.experimental.pallas import tpu as pltpu

C = 1280
DH = 64
GROUPS = 32
MEMBER = C // GROUPS
TAPS = 9
UNROLL = 8

EPS_RES = 1e-05
EPS_MID = 1e-06
EPS_LAYER = 1e-05

F32 = jnp.float32
BF16 = jnp.bfloat16


def dot(a, b, a_dim, b_dim, kind=F32):
    return lax.dot_general(
        a, b, (((a_dim,), (b_dim,)), ((), ())), preferred_element_type=F32
    ).astype(kind)


def swap(x, axis, mask):
    return lax.ppermute(x, axis, [(i, i ^ mask) for i in range(lax.axis_size(axis))])


def swap_half(x):
    return swap(x, "rows", 1)


def swap_core(x):
    return swap(x, "heads", 1)


def swap_far(x):
    return swap(x, "heads", 2)


def shift_image(x):
    n = lax.axis_size("rows")
    return lax.ppermute(x, "rows", [(i, (i + 2) % n) for i in range(n)])


def pair(own, other, place, axis):
    return jnp.where(
        place == 0,
        jnp.concatenate([own, other], axis=axis),
        jnp.concatenate([other, own], axis=axis),
    )


def pick(x, place, axis):
    return lax.dynamic_index_in_dim(x, place, axis, keepdims=False)


def part(x, place, count, axis=0):
    size = x.shape[axis] // count
    return lax.dynamic_slice_in_dim(x, place * size, size, axis)


class Place:
    def __init__(self):
        row = lax.axis_index("rows")
        head = lax.axis_index("heads")
        self.row = row
        self.half = row % 2
        self.image = row // 2
        self.images = lax.axis_size("rows") // 2
        self.core = head % 2
        self.far = head // 2
        self.head = head


def image_gather(at, chunk):
    n, size = at.images, chunk.shape[0]
    whole = jnp.zeros((n * size,) + chunk.shape[1:], chunk.dtype)

    def put(whole, chunk, step):
        start = lax.rem(at.image - step + n, n) * size
        return lax.dynamic_update_slice_in_dim(whole, chunk, start, 0)

    if n > UNROLL:

        def body(step, carry):
            whole, chunk = carry
            return put(whole, chunk, step), shift_image(chunk)

        return lax.fori_loop(0, n, body, (whole, chunk))[0]
    for step in range(n):
        whole = put(whole, chunk, step)
        if step < n - 1:
            chunk = shift_image(chunk)
    return whole


def rows_gather(at, chunk):
    n, size = at.images, chunk.shape[0]
    if n > UNROLL:
        own = image_gather(at, chunk)
        split = (n, 1) + chunk.shape
        both = pair(own.reshape(split), swap_half(own).reshape(split), at.half, 1)
        return both.reshape((2 * n * size,) + chunk.shape[1:])
    whole = jnp.zeros((2 * n * size,) + chunk.shape[1:], chunk.dtype)
    for step in range(n):
        start = lax.rem(at.image - step + n, n) * 2
        other = swap_half(chunk)
        whole = lax.dynamic_update_slice_in_dim(whole, chunk, (start + at.half) * size, 0)
        whole = lax.dynamic_update_slice_in_dim(whole, other, (start + 1 - at.half) * size, 0)
        if step < n - 1:
            chunk = shift_image(chunk)
    return whole


def image_scatter(at, blocks):
    n = at.images

    def local(step):
        return lax.dynamic_index_in_dim(
            blocks, lax.rem(at.image - 1 - step + 2 * n, n), 0, keepdims=False
        )

    def advance(step, moving):
        return shift_image(moving).astype(F32) + local(step + 1).astype(F32)

    moving = local(0)
    if n > UNROLL:
        moving = lax.fori_loop(
            0, n - 2, lambda step, value: advance(step, value).astype(blocks.dtype), moving
        )
    else:
        for step in range(n - 2):
            moving = advance(step, moving).astype(blocks.dtype)
    return advance(n - 2, moving)


def rows_scatter(at, grad):
    blocks = grad.reshape((at.images, 2, -1) + grad.shape[1:])
    other = swap_half(pick(blocks, 1 - at.half, 1))
    summed = (pick(blocks, at.half, 1).astype(F32) + other.astype(F32)).astype(BF16)
    return image_scatter(at, summed)


def rows_total(x, first=1):
    mask = first
    while mask < lax.axis_size("rows"):
        x = x + swap(x, "rows", mask)
        mask *= 2
    return x


def image_stack(at, x):
    x = x[None]
    mask = 1
    while mask < at.images:
        x = pair(x, swap(x, "rows", 2 * mask), (at.image // mask) % 2, 0)
        mask *= 2
    return x


def heads_scatter(at, grad):
    own = part(grad, at.core, 2).astype(F32)
    own = own + swap_core(part(grad, 1 - at.core, 2)).astype(F32)
    other = swap_far(part(own, 1 - at.far, 2).astype(BF16))
    return part(own, at.far, 2) + other.astype(F32)


def heads_gather(at, quarter):
    two = pair(quarter, swap_far(quarter), at.far, 0)
    return pair(two, swap_core(two), at.core, 0)


def to_tokens(at, x):
    other = swap_core(part(x, 1 - at.core, 2).astype(BF16)).astype(F32)
    x = pair(part(x, at.core, 2), other, at.core, 1)
    other = swap_far(part(x, 1 - at.far, 2).astype(BF16)).astype(F32)
    return pair(part(x, at.far, 2), other, at.far, 1)


def to_channels(at, x):
    wide = x.shape[1] // 2
    first, second = x[:, :wide], x[:, wide:]
    other = swap_far(jnp.where(at.far == 0, second, first))
    x = pair(jnp.where(at.far == 0, first, second), other, at.far, 0)
    wide = wide // 2
    first, second = x[:, :wide], x[:, wide:]
    other = swap_core(jnp.where(at.core == 0, second, first))
    return pair(jnp.where(at.core == 0, first, second), other, at.core, 0)


def channel_rows_gather(at, x):
    shape = x.shape
    x = pair(x[None], swap_far(x)[None], at.far, 0)
    x = pair(x[:, None], swap_core(x)[:, None], at.core, 1)
    return x.reshape((-1,) + shape[1:])


def channel_rows_scatter(at, x):
    blocks = x.reshape(2, 2, -1, x.shape[1])
    own = pick(blocks, at.core, 1).astype(F32)
    own = own + swap_core(pick(blocks, 1 - at.core, 1)).astype(F32)
    other = swap_far(pick(own, 1 - at.far, 0).astype(BF16))
    return pick(own, at.far, 0) + other.astype(F32)


def to_image(at, x):
    blocks = x.reshape(2, -1, x.shape[1])
    return pair(pick(blocks, at.half, 0), swap_half(pick(blocks, 1 - at.half, 0)), at.half, 1)


def from_image(at, x):
    return pair(
        part(x, at.half, 2, 1), swap_half(part(x, 1 - at.half, 2, 1)), at.half, 0
    )


def plane_gather(at, x):
    width, tokens = x.shape
    left, right = x[:, : tokens // 2], x[:, tokens // 2 :]
    left = pair(left[None], swap_half(left)[None], at.half, 0)
    right = pair(right[None], swap_far(right)[None], at.far, 0)
    left = pair(left[None], swap_far(left)[None], at.far, 0)
    right = pair(right[:, None], swap_half(right)[:, None], at.half, 1)
    x = jnp.concatenate([left, right], axis=3)
    x = pair(x[:, None], swap_core(x)[:, None], at.core, 1)
    return x.reshape(8 * width, tokens)


def plane_scatter(at, x):
    tokens = x.shape[1]
    blocks = x.reshape(2, 2, 2, -1, tokens)
    own = pick(blocks, at.core, 1).astype(F32)
    own = own + swap_core(pick(blocks, 1 - at.core, 1)).astype(F32)
    left, right = own[..., : tokens // 2], own[..., tokens // 2 :]
    left = pick(left, at.half, 1) + swap_half(pick(left, 1 - at.half, 1).astype(BF16)).astype(F32)
    right = pick(right, at.far, 0) + swap_far(pick(right, 1 - at.far, 0).astype(BF16)).astype(F32)
    left = pick(left, at.far, 0) + swap_far(pick(left, 1 - at.far, 0).astype(BF16)).astype(F32)
    right = pick(right, at.half, 0) + swap_half(pick(right, 1 - at.half, 0).astype(BF16)).astype(
        F32
    )
    return jnp.concatenate([left, right], axis=1)


def group_forward(inputs, gain, shift, epsilon):
    grouped = inputs.reshape(-1, MEMBER, inputs.shape[1])
    center = jnp.mean(grouped, axis=(1, 2), keepdims=True)
    inverse = lax.rsqrt(jnp.mean(jnp.square(grouped - center), axis=(1, 2), keepdims=True) + epsilon)
    normed = ((grouped - center) * inverse).reshape(inputs.shape)
    return normed * gain[:, None] + shift[:, None], (normed, inverse)


def group_backward(gradient, gain, stored):
    normed, inverse = stored
    shape = gradient.shape
    scaled = (gradient * gain[:, None]).reshape(-1, MEMBER, shape[1])
    flat = normed.reshape(scaled.shape)
    first = jnp.mean(scaled, axis=(1, 2), keepdims=True)
    second = jnp.mean(scaled * flat, axis=(1, 2), keepdims=True)
    back = (inverse * (scaled - first - flat * second)).reshape(shape)
    return back, [jnp.sum(gradient * normed, axis=1), jnp.sum(gradient, axis=1)]


def layer_forward(inputs, params):
    center = jnp.mean(inputs, axis=1, keepdims=True)
    inverse = lax.rsqrt(jnp.mean(jnp.square(inputs - center), axis=1, keepdims=True) + EPS_LAYER)
    normed = (inputs - center) * inverse
    return (normed * params[0] + params[1]).astype(BF16), (normed, inverse)


def layer_backward(gradient, params, stored):
    normed, inverse = stored
    scaled = gradient * params[0]
    first = jnp.mean(scaled, axis=1, keepdims=True)
    second = jnp.mean(scaled * normed, axis=1, keepdims=True)
    back = inverse * (scaled - first - normed * second)
    return back, [jnp.sum(gradient * normed, axis=0), jnp.sum(gradient, axis=0)]


def silu_slope(inputs):
    sigma = jax.nn.sigmoid(inputs)
    return sigma * (1.0 + inputs * (1.0 - sigma))


def tap_mask(shape, tap, columns):
    place = lax.broadcasted_iota(jnp.int32, shape, 1)
    line, column = place // columns, place % columns
    keep = None
    for value, step, count in (
        (line, tap // 3 - 1, shape[1] // columns),
        (column, tap % 3 - 1, columns),
    ):
        if step != 0:
            inside = value >= 1 if step < 0 else value <= count - 2
            keep = inside if keep is None else jnp.logical_and(keep, inside)
    return keep


def tap_offset(tap, columns):
    return (tap // 3 - 1) * columns + tap % 3 - 1


def tap_sum_kernel(columns, taps_ref, sum_ref):
    tokens = taps_ref.shape[2]
    total = taps_ref[4]
    for tap in range(TAPS):
        if tap != 4:
            moved = pltpu.roll(taps_ref[tap], -tap_offset(tap, columns) % tokens, 1)
            total = total + jnp.where(tap_mask(moved.shape, tap, columns), moved, 0.0)
    sum_ref[...] = total


def tap_sum(taps, columns):
    tokens = taps.shape[1]
    width = taps.shape[0] // TAPS
    block = 32
    return pl.pallas_call(
        lambda *refs: tap_sum_kernel(columns, *refs),
        grid=(width // block,),
        in_specs=[pl.BlockSpec((TAPS, block, tokens), lambda i: (0, i, 0))],
        out_specs=pl.BlockSpec((block, tokens), lambda i: (i, 0)),
        out_shape=jax.ShapeDtypeStruct((width, tokens), F32),
        compiler_params=pltpu.CompilerParams(vmem_limit_bytes=16 * 2**20),
        name="tap_sum",
    )(taps.reshape(TAPS, width, tokens))


def tap_spread_kernel(columns, grad_ref, taps_ref):
    tokens = grad_ref.shape[1]
    grad = grad_ref[...].astype(F32)
    for tap in range(TAPS):
        if tap == 4:
            taps_ref[tap] = grad_ref[...]
            continue
        moved = pltpu.roll(grad, tap_offset(tap, columns) % tokens, 1)
        keep = tap_mask(moved.shape, TAPS - 1 - tap, columns)
        taps_ref[tap] = jnp.where(keep, moved, 0.0).astype(taps_ref.dtype)


def tap_spread(grad, columns):
    width, tokens = grad.shape
    block = 32
    return pl.pallas_call(
        lambda *refs: tap_spread_kernel(columns, *refs),
        grid=(width // block,),
        in_specs=[pl.BlockSpec((block, tokens), lambda i: (i, 0))],
        out_specs=pl.BlockSpec((TAPS, block, tokens), lambda i: (0, i, 0)),
        out_shape=jax.ShapeDtypeStruct((TAPS, width, tokens), BF16),
        compiler_params=pltpu.CompilerParams(vmem_limit_bytes=16 * 2**20),
        name="tap_spread",
    )(grad).reshape(TAPS * width, tokens)


def conv_weights(at, kernel):
    inputs, outputs = kernel.shape[2:]
    halves = kernel.reshape(TAPS, inputs, 2, outputs // 2).transpose(2, 1, 0, 3)
    halves = halves.reshape(2, inputs, -1)
    other = swap_half(pick(halves, 1 - at.half, 0))
    return image_gather(at, pair(pick(halves, at.half, 0), other, at.half, 0))


def conv_weights_back(at, grad, inputs):
    total = image_scatter(at, grad.reshape(at.images, 2 * inputs, -1))
    other = swap_half(part(total, 1 - at.half, 2).astype(BF16)).astype(F32)
    own = part(total, at.half, 2).reshape(inputs, TAPS, -1)
    grad = pair(own, other.reshape(inputs, TAPS, -1), at.half, 2)
    return grad.transpose(1, 0, 2).reshape(3, 3, inputs, -1)


def by_heads(x):
    return x.reshape(x.shape[0], -1, DH)


def attend(queries, blocks):
    q_heads = by_heads(queries)
    scores = [
        jnp.einsum("qhd,khd->hqk", q_heads, by_heads(keys), preferred_element_type=F32)
        * (1.0 / math.sqrt(DH))
        for keys, values in blocks
    ]
    peak = scores[0].max(axis=-1, keepdims=True)
    for one in scores[1:]:
        peak = jnp.maximum(peak, one.max(axis=-1, keepdims=True))
    raised = [jnp.exp(one - peak) for one in scores]
    total = sum(one.sum(axis=-1, keepdims=True) for one in raised)
    joined = sum(
        jnp.einsum(
            "hqk,khd->qhd",
            (one / total).astype(BF16),
            by_heads(values),
            preferred_element_type=F32,
        )
        for one, (keys, values) in zip(raised, blocks)
    )
    return joined.reshape(queries.shape).astype(BF16), peak + jnp.log(total)


def attend_back(grad_out, queries, blocks, log_total):
    scaling = 1.0 / math.sqrt(DH)
    q_heads, g_heads = by_heads(queries), by_heads(grad_out)
    probs, slopes = [], []
    for keys, values in blocks:
        scores = jnp.einsum("qhd,khd->hqk", q_heads, by_heads(keys), preferred_element_type=F32)
        probs.append(jnp.exp(scores * scaling - log_total))
        slopes.append(
            jnp.einsum("qhd,khd->hqk", g_heads, by_heads(values), preferred_element_type=F32)
        )
    center = sum(
        jnp.sum(one * slope, axis=-1, keepdims=True) for one, slope in zip(probs, slopes)
    )
    grad_query, grad_blocks = 0.0, []
    for one, slope, (keys, values) in zip(probs, slopes, blocks):
        grad_scores = (one * (slope - center)).astype(BF16)
        grad_query = grad_query + jnp.einsum(
            "hqk,khd->qhd", grad_scores, by_heads(keys), preferred_element_type=F32
        )
        grad_keys = scaling * jnp.einsum(
            "hqk,qhd->khd", grad_scores, q_heads, preferred_element_type=F32
        )
        grad_values = jnp.einsum(
            "hqk,qhd->khd", one.astype(BF16), g_heads, preferred_element_type=F32
        )
        grad_blocks.append(
            jnp.concatenate(
                [grad_keys.reshape(keys.shape), grad_values.reshape(values.shape)], axis=1
            )
        )
    return (grad_query * scaling).reshape(queries.shape).astype(BF16), grad_blocks


def on_device(
    latents,
    text,
    step_count,
    time_index,
    conv1_w,
    conv2_w,
    time_w,
    proj_in_w,
    qkv_w,
    self_out_w,
    cross_q_w,
    cross_kv_w,
    cross_out_w,
    ff_in_w,
    ff_out_w,
    proj_out_w,
    gn_params,
    ln_params,
    biases,
    ff_bias,
    cotangent,
):
    at = Place()
    columns = latents.shape[2]
    width = latents.shape[3]
    tokens = latents.shape[1] * columns
    half = width // 2
    inputs = time_w.shape[0]
    hidden = ff_in_w.shape[2]

    conv_one = conv_weights(at, conv1_w)
    conv_two = conv_weights(at, conv2_w)
    w_first = rows_gather(
        at,
        jnp.concatenate([qkv_w[:, 1], qkv_w[:, 2], qkv_w[:, 0], proj_in_w], axis=1),
    )
    w_kvq, w_in = w_first[:, : 3 * width], w_first[:, 3 * width :]
    w_second = rows_gather(
        at, jnp.concatenate([self_out_w.T, cross_q_w, cross_out_w.T, proj_out_w], axis=1)
    )
    w_self, w_query, w_cross, w_out = (
        w_second[:, i * width : (i + 1) * width] for i in range(4)
    )
    w_value = rows_gather(at, ff_in_w[:, 0])
    w_gate = rows_gather(at, ff_in_w[:, 1])
    w_narrow = rows_gather(at, ff_out_w.T)

    own_params = jnp.concatenate([ln_params.reshape(6, width), biases[4:7]], axis=0)
    wide = pair(own_params, swap_core(own_params), at.core, 1)
    wide = pair(wide, swap_far(wide), at.far, 1)
    ln_wide, bias_self, bias_cross, bias_narrow = wide[:6].reshape(3, 2, C), wide[6], wide[7], wide[8]
    gn_own = part(gn_params, at.half, 2, 2)
    bias_own = part(biases, at.half, 2, 1)

    images = step_count.shape[0]
    moment = (999 - 1000 * time_index // step_count).astype(F32)
    half_width = C // 2
    channel = at.row * inputs + jnp.arange(inputs)
    frequency = jnp.exp(-math.log(10000.0) * (channel % half_width).astype(F32) / half_width)
    angles = moment[:, None] * frequency[None, :]
    embedding = jnp.where(channel[None, :] < half_width, jnp.cos(angles), jnp.sin(angles))
    temb_low = jax.nn.silu(embedding).astype(BF16)
    shift_all = rows_total(jnp.dot(temb_low, time_w, preferred_element_type=F32))
    shift_time = lax.dynamic_index_in_dim(shift_all, at.image, 0, keepdims=False)
    shift_time = part(shift_time, at.half, 2) + bias_own[1]

    text_own = part(text, at.row, lax.axis_size("rows"), 2)
    pair_w = cross_kv_w.reshape(cross_kv_w.shape[0], -1)
    kv_part = jnp.einsum("isc,cd->isd", text_own, pair_w, preferred_element_type=F32)
    kv_part = (kv_part + swap_half(kv_part.astype(BF16)).astype(F32)).astype(BF16)
    cross_kv = image_scatter(at, kv_part).astype(BF16)
    cross_keys, cross_values = cross_kv[:, :width], cross_kv[:, width:]

    source = to_image(at, latents.reshape(tokens, width).T).astype(F32)
    cot_rows = cotangent.reshape(tokens, width)
    cot_image = to_image(at, cot_rows.T).astype(F32)
    norm_one, stored_one = group_forward(source, gn_own[0, 0], gn_own[0, 1], EPS_RES)
    act_one = plane_gather(at, jax.nn.silu(norm_one).astype(BF16))
    hidden_two = tap_sum(dot(conv_one, act_one, 0, 0), columns)
    hidden_two = hidden_two + (bias_own[0] + shift_time)[:, None]
    norm_two, stored_two = group_forward(hidden_two, gn_own[1, 0], gn_own[1, 1], EPS_RES)
    act_two = plane_gather(at, jax.nn.silu(norm_two).astype(BF16))
    resid = source + tap_sum(dot(conv_two, act_two, 0, 0), columns) + bias_own[2][:, None]
    norm_three, stored_three = group_forward(resid, gn_own[2, 0], gn_own[2, 1], EPS_MID)
    gin = channel_rows_gather(at, from_image(at, norm_three.astype(BF16)))
    resid_own = from_image(at, resid)

    stream_zero = to_tokens(at, dot(gin, w_in, 0, 0) + biases[3])
    low_one, stored_ln_one = layer_forward(stream_zero, ln_wide[0])
    n_one = heads_gather(at, low_one)
    kv_own = dot(n_one, w_kvq[:, : 2 * width], 1, 0, BF16)
    kv_other = swap_half(kv_own)
    queries = dot(n_one, w_kvq[:, 2 * width :], 1, 0, BF16)
    self_blocks = [(kv[:, :width], kv[:, width:]) for kv in (kv_own, kv_other)]
    attended, log_self = attend(queries, self_blocks)
    stream_one = stream_zero + heads_scatter(at, dot(attended, w_self, 1, 1, BF16)) + bias_self

    low_two, stored_ln_two = layer_forward(stream_one, ln_wide[1])
    n_two = heads_gather(at, low_two)
    cross_query = dot(n_two, w_query, 1, 0, BF16)
    cross_blocks = [(cross_keys, cross_values)]
    cross_att, log_cross = attend(cross_query, cross_blocks)
    stream_two = stream_one + heads_scatter(at, dot(cross_att, w_cross, 1, 1, BF16)) + bias_cross

    low_three, stored_ln_three = layer_forward(stream_two, ln_wide[2])
    n_three = heads_gather(at, low_three)
    value_in = dot(n_three, w_value, 1, 0) + ff_bias[0]
    gate_in = dot(n_three, w_gate, 1, 0) + ff_bias[1]
    cdf = 0.5 * (1.0 + lax.erf(gate_in / math.sqrt(2.0)))
    gelu = gate_in * cdf
    mixed = (value_in * gelu).astype(BF16)
    stream_three = stream_two + heads_scatter(at, dot(mixed, w_narrow, 1, 1, BF16)) + bias_narrow
    three = heads_gather(at, stream_three.astype(BF16))
    result = resid_own + (dot(w_out, three, 0, 1) + biases[7][:, None])
    output = result.astype(BF16).T.reshape(latents.shape)

    out_grad = dot(three, cot_rows, 0, 0, BF16)
    bias_seven = jnp.sum(cot_rows.astype(F32), axis=0)
    grad_three = heads_scatter(at, dot(cot_rows, w_out, 1, 1, BF16))
    low_ff = grad_three.astype(BF16)
    grad_ff = heads_gather(at, low_ff)
    narrow_grad = dot(grad_ff, mixed, 0, 0, BF16)
    grad_mixed = dot(grad_ff, w_narrow, 1, 0, BF16).astype(F32)
    pdf = jnp.exp(-0.5 * gate_in * gate_in) / math.sqrt(2.0 * math.pi)
    grad_value = (grad_mixed * gelu).astype(BF16)
    grad_gate = (grad_mixed * value_in * (cdf + gate_in * pdf)).astype(BF16)
    ffbias_grad = jnp.stack(
        [jnp.sum(grad_value.astype(F32), axis=0), jnp.sum(grad_gate.astype(F32), axis=0)]
    )
    value_grad = dot(n_three, grad_value, 0, 0, BF16)
    gate_grad = dot(n_three, grad_gate, 0, 0, BF16)
    grad_ln = heads_scatter(
        at, (dot(grad_value, w_value, 1, 1) + dot(grad_gate, w_gate, 1, 1)).astype(BF16)
    )
    back, ln_grad_three = layer_backward(grad_ln, ln_wide[2], stored_ln_three)
    grad_two = grad_three + back

    low_cross = grad_two.astype(BF16)
    grad_cross = heads_gather(at, low_cross)
    cross_grad = dot(grad_cross, cross_att, 0, 0, BF16)
    grad_cross_att = dot(grad_cross, w_cross, 1, 0, BF16)
    grad_cq, (grad_ckv,) = attend_back(grad_cross_att, cross_query, cross_blocks, log_cross)
    query_grad = dot(n_two, grad_cq, 0, 0, BF16)
    grad_ckv = (grad_ckv + swap_half(grad_ckv.astype(BF16)).astype(F32)).astype(BF16)
    grad_ckv = image_gather(at, grad_ckv[None])
    pair_grad = jnp.einsum("isc,isd->cd", text_own, grad_ckv, preferred_element_type=F32)
    grad_ln = heads_scatter(at, dot(grad_cq, w_query, 1, 1, BF16))
    back, ln_grad_two = layer_backward(grad_ln, ln_wide[1], stored_ln_two)
    grad_one = grad_two + back

    low_self = grad_one.astype(BF16)
    grad_self = heads_gather(at, low_self)
    self_grad = dot(grad_self, attended, 0, 0, BF16)
    grad_attended = dot(grad_self, w_self, 1, 0, BF16)
    grad_q, (grad_kv, grad_kv_other) = attend_back(grad_attended, queries, self_blocks, log_self)
    grad_kv = (grad_kv + swap_half(grad_kv_other.astype(BF16)).astype(F32)).astype(BF16)
    grad_kvq = jnp.concatenate([grad_kv, grad_q], axis=1)
    kvq_grad = dot(n_one, grad_kvq, 0, 0, BF16)
    grad_ln = heads_scatter(at, dot(grad_kvq, w_kvq, 1, 1, BF16))
    back, ln_grad_one = layer_backward(grad_ln, ln_wide[0], stored_ln_one)
    grad_zero = to_channels(at, (grad_one + back).astype(BF16))
    in_grad = dot(gin, grad_zero, 1, 0, BF16)
    bias_three = jnp.sum(grad_zero.astype(F32), axis=0)
    grad_gin = channel_rows_scatter(at, dot(w_in, grad_zero, 1, 1, BF16))

    own_half = pick(grad_gin.reshape(2, half, tokens), at.half, 0)
    other_half = pick(grad_gin.reshape(2, half, tokens), 1 - at.half, 0)
    grad_gin = pair(own_half, swap_half(other_half.astype(BF16)).astype(F32), at.half, 1)
    back, gn_grad_three = group_backward(grad_gin, gn_own[2, 0], stored_three)
    grad_resid = cot_image + back
    grad_c_two = grad_resid.astype(BF16)
    bias_two = jnp.sum(grad_c_two.astype(F32), axis=1)
    spread_two = tap_spread(grad_c_two, columns)
    grad_act = plane_scatter(at, dot(conv_two, spread_two, 1, 0, BF16))
    conv_two_grad = dot(act_two, spread_two, 1, 1, BF16)
    grad_hidden, gn_grad_two = group_backward(
        grad_act * silu_slope(norm_two), gn_own[1, 0], stored_two
    )
    image_sum = jnp.sum(grad_hidden, axis=1)
    grad_c_one = grad_hidden.astype(BF16)
    bias_zero = jnp.sum(grad_c_one.astype(F32), axis=1)
    spread_one = tap_spread(grad_c_one, columns)
    grad_act = plane_scatter(at, dot(conv_one, spread_one, 1, 0, BF16))
    conv_one_grad = dot(act_one, spread_one, 1, 1, BF16)
    back, gn_grad_one = group_backward(
        grad_act * silu_slope(norm_one), gn_own[0, 0], stored_one
    )
    latents_grad = from_image(at, grad_resid + back).T.reshape(latents.shape)

    second = rows_scatter(
        at, jnp.concatenate([self_grad, query_grad, cross_grad, out_grad], axis=1)
    )
    narrow = rows_scatter(at, narrow_grad)
    value = rows_scatter(at, value_grad)
    gate = rows_scatter(at, gate_grad)
    first = rows_scatter(at, jnp.concatenate([kvq_grad, in_grad], axis=1))
    conv_two_out = conv_weights_back(at, conv_two_grad, inputs)
    conv_one_out = conv_weights_back(at, conv_one_grad, inputs)

    token_sums = jnp.stack(
        ln_grad_one
        + ln_grad_two
        + ln_grad_three
        + [jnp.sum(low.astype(F32), axis=0) for low in (low_self, low_cross, low_ff)]
    )
    wide_half = C // 2
    keep = jnp.where(at.far == 0, token_sums[:, :wide_half], token_sums[:, wide_half:])
    send = jnp.where(at.far == 0, token_sums[:, wide_half:], token_sums[:, :wide_half])
    keep = keep + swap_far(send)
    own = jnp.where(at.core == 0, keep[:, :width], keep[:, width:])
    send = jnp.where(at.core == 0, keep[:, width:], keep[:, :width])
    own = own + swap_core(send)
    own = jnp.concatenate(
        [own, bias_three[None], bias_seven[None], ffbias_grad.reshape(-1, width)], axis=0
    )
    own = rows_total(own)
    ln_total = own[:6].reshape(3, 2, width)
    ffbias_total = own[11:].reshape(2, hidden)
    image_sums = jnp.stack(
        gn_grad_one + gn_grad_two + gn_grad_three + [bias_zero, image_sum, bias_two]
    )
    image_sums = image_stack(at, image_sums)
    image_sums = pair(image_sums, swap_half(image_sums), at.half, 2)
    totals = jnp.sum(image_sums, axis=0)
    gn_total = totals[:6].reshape(3, 2, width)
    bias_total = jnp.concatenate([totals[6:9], own[9:10], own[6:9], own[10:11]], axis=0)
    time_grad = lax.dot_general(
        temb_low.astype(F32),
        image_sums[:, 7],
        (((0,), (0,)), ((), ())),
        precision=lax.Precision.HIGHEST,
        preferred_element_type=F32,
    )

    cut = [i * width for i in range(5)]
    return (
        output,
        latents_grad,
        conv_one_out,
        conv_two_out,
        time_grad,
        first[:, cut[3] : cut[4]],
        jnp.stack([first[:, cut[2] : cut[3]], first[:, : cut[1]], first[:, cut[1] : cut[2]]], axis=1),
        second[:, : cut[1]].T,
        second[:, cut[1] : cut[2]],
        pair_grad.reshape(cross_kv_w.shape),
        second[:, cut[2] : cut[3]].T,
        jnp.stack([value, gate], axis=1),
        narrow.T,
        second[:, cut[3] : cut[4]],
        gn_total,
        ln_total,
        bias_total,
        ffbias_total,
    )


def solution(mesh):
    return jax.shard_map(
        on_device,
        mesh=mesh,
        in_specs=(
            P("rows", None, None, "heads"),
            P(),
            P(),
            P(),
            P(None, None, "rows", "heads"),
            P(None, None, "rows", "heads"),
            P("rows", "heads"),
            P("rows", "heads"),
            P("rows", None, "heads"),
            P("heads", "rows"),
            P("rows", "heads"),
            P("rows", None, "heads"),
            P("heads", "rows"),
            P("rows", None, "heads"),
            P("heads", "rows"),
            P("rows", "heads"),
            P(None, None, "heads"),
            P(None, None, "heads"),
            P(None, "heads"),
            P(None, "heads"),
            P("rows", None, None, "heads"),
        ),
        out_specs=(
            P("rows", None, None, "heads"),
            P("rows", None, None, "heads"),
            P(None, None, "rows", "heads"),
            P(None, None, "rows", "heads"),
            P("rows", "heads"),
            P("rows", "heads"),
            P("rows", None, "heads"),
            P("heads", "rows"),
            P("rows", "heads"),
            P("rows", None, "heads"),
            P("heads", "rows"),
            P("rows", None, "heads"),
            P("heads", "rows"),
            P("rows", "heads"),
            P(None, None, "heads"),
            P(None, None, "heads"),
            P(None, "heads"),
            P(None, "heads"),
        ),
        check_vma=False,
    )
```

```python
import math

import jax
import jax.numpy as jnp
from jax import lax
from jax.experimental import pallas as pl
from jax.experimental.layout import Layout, with_layout_constraint
from jax.sharding import PartitionSpec as P
from jax.experimental.pallas import tpu as pltpu

C = 1280
DH = 64
GROUPS = 32
MEMBER = C // GROUPS
TAPS = 9
UNROLL = 8

EPS_RES = 1e-05
EPS_MID = 1e-06
EPS_LAYER = 1e-05

F32 = jnp.float32
BF16 = jnp.bfloat16


def dot(a, b, a_dim, b_dim, kind=F32):
    return lax.dot_general(
        a, b, (((a_dim,), (b_dim,)), ((), ())), preferred_element_type=F32
    ).astype(kind)


def row_major(x):
    return with_layout_constraint(x, Layout(tuple(range(x.ndim))))


def swap(x, axis, mask):
    return lax.ppermute(x, axis, [(i, i ^ mask) for i in range(lax.axis_size(axis))])


def swap_half(x):
    return swap(x, "rows", 1)


def swap_core(x):
    return swap(x, "heads", 1)


def swap_far(x):
    return swap(x, "heads", 2)


def shift_image(x, images=1):
    n = lax.axis_size("rows")
    return lax.ppermute(x, "rows", [(i, (i + 2 * images) % n) for i in range(n)])


def pair(own, other, place, axis):
    return jnp.where(
        place == 0,
        jnp.concatenate([own, other], axis=axis),
        jnp.concatenate([other, own], axis=axis),
    )


def pick(x, place, axis):
    return lax.dynamic_index_in_dim(x, place, axis, keepdims=False)


def part(x, place, count, axis=0):
    size = x.shape[axis] // count
    return lax.dynamic_slice_in_dim(x, place * size, size, axis)


class Place:
    def __init__(self):
        row = lax.axis_index("rows")
        head = lax.axis_index("heads")
        self.row = row
        self.half = row % 2
        self.image = row // 2
        self.images = lax.axis_size("rows") // 2
        self.core = head % 2
        self.far = head // 2
        self.head = head


def image_gather(at, chunk):
    n, size = at.images, chunk.shape[0]
    whole = jnp.zeros((n * size,) + chunk.shape[1:], chunk.dtype)

    def put(whole, chunk, step):
        start = lax.rem(at.image - step + n, n) * size
        return lax.dynamic_update_slice_in_dim(whole, chunk, start, 0)

    if n > UNROLL:

        def body(step, carry):
            whole, chunk = carry
            return put(whole, chunk, step), shift_image(chunk)

        return lax.fori_loop(0, n, body, (whole, chunk))[0]
    for step in range(n):
        whole = put(whole, chunk, step)
        if step < n - 1:
            chunk = shift_image(chunk)
    return whole


def rows_gather(chunk):
    return lax.all_gather(chunk, "rows", axis=0, tiled=True)


def rows_scatter(grad):
    return lax.psum_scatter(grad, "rows", scatter_dimension=0, tiled=True).astype(F32)


def small_gather(at, x):
    n = at.images
    if n > UNROLL:
        return image_gather(at, x[None])
    whole = jnp.zeros((n,) + x.shape, x.dtype)
    for step in range(n):
        other = shift_image(x, step) if step else x
        start = lax.rem(at.image - step + n, n)
        whole = lax.dynamic_update_index_in_dim(whole, other, start, 0)
    return whole


def small_scatter(at, blocks):
    n = at.images
    if n > UNROLL:
        return image_scatter(at, blocks)
    total = lax.dynamic_index_in_dim(blocks, at.image, 0, keepdims=False).astype(F32)
    for step in range(1, n):
        block = lax.dynamic_index_in_dim(
            blocks, lax.rem(at.image + step, n), 0, keepdims=False
        )
        total = total + shift_image(block, step).astype(F32)
    return total


def image_scatter(at, blocks):
    n = at.images

    def local(step):
        return lax.dynamic_index_in_dim(
            blocks, lax.rem(at.image - 1 - step + 2 * n, n), 0, keepdims=False
        )

    def advance(step, moving):
        return shift_image(moving).astype(F32) + local(step + 1).astype(F32)

    moving = local(0)
    if n > UNROLL:
        moving = lax.fori_loop(
            0, n - 2, lambda step, value: advance(step, value).astype(blocks.dtype), moving
        )
    else:
        for step in range(n - 2):
            moving = advance(step, moving).astype(blocks.dtype)
    return advance(n - 2, moving)


def image_spread(at, chunk):
    if at.images != 4:
        return image_gather(at, chunk)
    size = chunk.shape[0]
    up, down = shift_image(chunk, 1), shift_image(chunk, 3)
    far = (shift_image(up[: size // 2], 1), shift_image(down[size // 2 :], 3))
    whole = jnp.concatenate([chunk] * 4, axis=0)
    for move, block in ((3, up), (1, down), (2, jnp.concatenate(far, axis=0))):
        start = lax.rem(at.image + move, 4) * size
        whole = lax.dynamic_update_slice_in_dim(whole, block, start, 0)
    return whole


def add_low(a, b):
    return (a.astype(F32) + b.astype(F32)).astype(BF16)


def image_total(at, blocks):
    if at.images != 4:
        return image_scatter(at, blocks)

    def local(move):
        place = lax.rem(at.image + move, 4)
        return lax.dynamic_index_in_dim(blocks, place, 0, keepdims=False)

    size = blocks.shape[1] // 2
    far, up, down = local(2), local(1), local(3)
    first, second = shift_image(far[:size], 1), shift_image(far[size:], 3)
    up = jnp.concatenate([add_low(up[:size], first), up[size:]], axis=0)
    down = jnp.concatenate([down[:size], add_low(down[size:], second)], axis=0)
    up, down = shift_image(up, 1), shift_image(down, 3)
    return local(0).astype(F32) + up.astype(F32) + down.astype(F32)


def rows_total(x, first=1):
    mask = first
    while mask < lax.axis_size("rows"):
        x = x + swap(x, "rows", mask)
        mask *= 2
    return x


def image_stack(at, x):
    x = x[None]
    mask = 1
    while mask < at.images:
        x = pair(x, swap(x, "rows", 2 * mask), (at.image // mask) % 2, 0)
        mask *= 2
    return x


def heads_scatter(at, grad):
    own = part(grad, at.core, 2).astype(F32)
    own = own + swap_core(part(grad, 1 - at.core, 2)).astype(F32)
    other = swap_far(part(own, 1 - at.far, 2).astype(BF16))
    return part(own, at.far, 2) + other.astype(F32)


def heads_gather(at, quarter):
    two = pair(quarter, swap_far(quarter), at.far, 0)
    return pair(two, swap_core(two), at.core, 0)


def to_tokens(at, x):
    other = swap_core(part(x, 1 - at.core, 2).astype(BF16)).astype(F32)
    x = pair(part(x, at.core, 2), other, at.core, 1)
    other = swap_far(part(x, 1 - at.far, 2).astype(BF16)).astype(F32)
    return pair(part(x, at.far, 2), other, at.far, 1)


def to_channels(at, x):
    wide = x.shape[1] // 2
    first, second = x[:, :wide], x[:, wide:]
    other = swap_far(jnp.where(at.far == 0, second, first))
    x = pair(jnp.where(at.far == 0, first, second), other, at.far, 0)
    wide = wide // 2
    first, second = x[:, :wide], x[:, wide:]
    other = swap_core(jnp.where(at.core == 0, second, first))
    return pair(jnp.where(at.core == 0, first, second), other, at.core, 0)


def channel_rows_gather(at, x):
    shape = x.shape
    x = pair(x[None], swap_far(x)[None], at.far, 0)
    x = pair(x[:, None], swap_core(x)[:, None], at.core, 1)
    return x.reshape((-1,) + shape[1:])


def channel_rows_scatter(at, x):
    blocks = x.reshape(2, 2, -1, x.shape[1])
    own = pick(blocks, at.core, 1).astype(F32)
    own = own + swap_core(pick(blocks, 1 - at.core, 1)).astype(F32)
    other = swap_far(pick(own, 1 - at.far, 0).astype(BF16))
    return pick(own, at.far, 0) + other.astype(F32)


def to_image(at, x):
    blocks = x.reshape(2, -1, x.shape[1])
    return pair(pick(blocks, at.half, 0), swap_half(pick(blocks, 1 - at.half, 0)), at.half, 1)


def from_image(at, x):
    return pair(
        part(x, at.half, 2, 1), swap_half(part(x, 1 - at.half, 2, 1)), at.half, 0
    )


def plane_gather(at, x):
    width, tokens = x.shape
    left, right = x[:, : tokens // 2], x[:, tokens // 2 :]
    left = pair(left[None], swap_half(left)[None], at.half, 0)
    right = pair(right[None], swap_far(right)[None], at.far, 0)
    left = pair(left[None], swap_far(left)[None], at.far, 0)
    right = pair(right[:, None], swap_half(right)[:, None], at.half, 1)
    x = jnp.concatenate([left, right], axis=3)
    x = pair(x[:, None], swap_core(x)[:, None], at.core, 1)
    return x.reshape(8 * width, tokens)


def plane_scatter(at, x):
    tokens = x.shape[1]
    blocks = x.reshape(2, 2, 2, -1, tokens)
    own = pick(blocks, at.core, 1).astype(F32)
    own = own + swap_core(pick(blocks, 1 - at.core, 1)).astype(F32)
    left, right = own[..., : tokens // 2], own[..., tokens // 2 :]
    left = pick(left, at.half, 1) + swap_half(pick(left, 1 - at.half, 1).astype(BF16)).astype(F32)
    right = pick(right, at.far, 0) + swap_far(pick(right, 1 - at.far, 0).astype(BF16)).astype(F32)
    left = pick(left, at.far, 0) + swap_far(pick(left, 1 - at.far, 0).astype(BF16)).astype(F32)
    right = pick(right, at.half, 0) + swap_half(pick(right, 1 - at.half, 0).astype(BF16)).astype(
        F32
    )
    return jnp.concatenate([left, right], axis=1)


def group_forward(inputs, gain, shift, epsilon):
    grouped = inputs.reshape(-1, MEMBER, inputs.shape[1])
    center = jnp.mean(grouped, axis=(1, 2), keepdims=True)
    inverse = lax.rsqrt(jnp.mean(jnp.square(grouped - center), axis=(1, 2), keepdims=True) + epsilon)
    normed = ((grouped - center) * inverse).reshape(inputs.shape)
    return normed * gain[:, None] + shift[:, None], (normed, inverse)


def group_backward(gradient, gain, stored):
    normed, inverse = stored
    shape = gradient.shape
    scaled = (gradient * gain[:, None]).reshape(-1, MEMBER, shape[1])
    flat = normed.reshape(scaled.shape)
    first = jnp.mean(scaled, axis=(1, 2), keepdims=True)
    second = jnp.mean(scaled * flat, axis=(1, 2), keepdims=True)
    back = (inverse * (scaled - first - flat * second)).reshape(shape)
    return back, [jnp.sum(gradient * normed, axis=1), jnp.sum(gradient, axis=1)]


def layer_forward(inputs, params):
    center = jnp.mean(inputs, axis=1, keepdims=True)
    inverse = lax.rsqrt(jnp.mean(jnp.square(inputs - center), axis=1, keepdims=True) + EPS_LAYER)
    normed = (inputs - center) * inverse
    return (normed * params[0] + params[1]).astype(BF16), (normed, inverse)


def layer_backward(gradient, params, stored):
    normed, inverse = stored
    scaled = gradient * params[0]
    first = jnp.mean(scaled, axis=1, keepdims=True)
    second = jnp.mean(scaled * normed, axis=1, keepdims=True)
    back = inverse * (scaled - first - normed * second)
    return back, [jnp.sum(gradient * normed, axis=0), jnp.sum(gradient, axis=0)]


def silu_slope(inputs):
    sigma = jax.nn.sigmoid(inputs)
    return sigma * (1.0 + inputs * (1.0 - sigma))


def tap_mask(shape, tap, columns):
    place = lax.broadcasted_iota(jnp.int32, shape, 1)
    line, column = place // columns, place % columns
    keep = None
    for value, step, count in (
        (line, tap // 3 - 1, shape[1] // columns),
        (column, tap % 3 - 1, columns),
    ):
        if step != 0:
            inside = value >= 1 if step < 0 else value <= count - 2
            keep = inside if keep is None else jnp.logical_and(keep, inside)
    return keep


def tap_offset(tap, columns):
    return (tap // 3 - 1) * columns + tap % 3 - 1


def conv_kernel(columns, weights_ref, acts_ref, sum_ref, taps_ref):
    width, tokens = sum_ref.shape
    acts = acts_ref[...]
    for start in range(0, TAPS * width, 256):
        cut = slice(start, min(start + 256, TAPS * width))
        taps_ref[cut, :] = lax.dot_general(
            weights_ref[:, cut], acts, (((0,), (0,)), ((), ())), preferred_element_type=F32
        )
    for start in range(0, width, 32):
        total = taps_ref[4 * width + start : 4 * width + start + 32, :]
        for tap in range(TAPS):
            if tap != 4:
                taps = taps_ref[tap * width + start : tap * width + start + 32, :]
                moved = pltpu.roll(taps, -tap_offset(tap, columns) % tokens, 1)
                total = total + jnp.where(tap_mask(moved.shape, tap, columns), moved, 0.0)
        sum_ref[start : start + 32, :] = total


def conv_forward(weights, acts, columns):
    tokens = acts.shape[1]
    width = weights.shape[1] // TAPS
    return pl.pallas_call(
        lambda *refs: conv_kernel(columns, *refs),
        in_specs=[pl.BlockSpec(memory_space=pltpu.VMEM)] * 2,
        out_specs=pl.BlockSpec(memory_space=pltpu.VMEM),
        out_shape=jax.ShapeDtypeStruct((width, tokens), F32),
        scratch_shapes=[pltpu.VMEM((TAPS * width, tokens), F32)],
        compiler_params=pltpu.CompilerParams(vmem_limit_bytes=40 * 2**20),
        cost_estimate=pl.CostEstimate(
            flops=2 * weights.size * tokens, bytes_accessed=2 * weights.size, transcendentals=0
        ),
        name="conv_forward",
    )(weights, acts)


def tap_spread_kernel(columns, grad_ref, taps_ref):
    tokens = grad_ref.shape[1]
    grad = grad_ref[...].astype(F32)
    for tap in range(TAPS):
        if tap == 4:
            taps_ref[tap] = grad_ref[...]
            continue
        moved = pltpu.roll(grad, tap_offset(tap, columns) % tokens, 1)
        keep = tap_mask(moved.shape, TAPS - 1 - tap, columns)
        taps_ref[tap] = jnp.where(keep, moved, 0.0).astype(taps_ref.dtype)


def tap_spread(grad, columns):
    width, tokens = grad.shape
    block = 32
    return pl.pallas_call(
        lambda *refs: tap_spread_kernel(columns, *refs),
        grid=(width // block,),
        in_specs=[pl.BlockSpec((block, tokens), lambda i: (i, 0))],
        out_specs=pl.BlockSpec((TAPS, block, tokens), lambda i: (0, i, 0)),
        out_shape=jax.ShapeDtypeStruct((TAPS, width, tokens), BF16),
        compiler_params=pltpu.CompilerParams(vmem_limit_bytes=16 * 2**20),
        name="tap_spread",
    )(grad).reshape(TAPS * width, tokens)


def pack_kernel(kernel_ref, halves_ref):
    half = kernel_ref.shape[2] // 2
    taps = [kernel_ref[tap].astype(F32) for tap in range(TAPS)]
    for side in range(2):
        row = jnp.concatenate([tap[:, side * half : (side + 1) * half] for tap in taps], axis=1)
        halves_ref[side] = row.astype(halves_ref.dtype)


def pack(kernel):
    taps, inputs, outputs = kernel.shape
    block = 32 if inputs % 32 == 0 else inputs
    return pl.pallas_call(
        pack_kernel,
        grid=(inputs // block,),
        in_specs=[pl.BlockSpec((taps, block, outputs), lambda i: (0, i, 0))],
        out_specs=pl.BlockSpec((2, block, taps * outputs // 2), lambda i: (0, i, 0)),
        out_shape=jax.ShapeDtypeStruct((2, inputs, taps * outputs // 2), kernel.dtype),
        compiler_params=pltpu.CompilerParams(vmem_limit_bytes=16 * 2**20),
        name="conv_pack",
    )(kernel)


def unpack_kernel(side_ref, own_ref, other_ref, kernel_ref):
    half = kernel_ref.shape[2] // 2
    first = side_ref[0] == 0
    own, other = own_ref[...], other_ref[...].astype(F32)
    low, high = jnp.where(first, own, other), jnp.where(first, other, own)
    for tap in range(TAPS):
        cut = slice(tap * half, (tap + 1) * half)
        kernel_ref[tap] = jnp.concatenate([low[:, cut], high[:, cut]], axis=1)


def unpack(side, own, other):
    inputs, width = own.shape
    outputs = 2 * width // TAPS
    block = 32 if inputs % 32 == 0 else inputs
    rows = pl.BlockSpec((block, width), lambda i: (i, 0))
    return pl.pallas_call(
        unpack_kernel,
        grid=(inputs // block,),
        in_specs=[pl.BlockSpec(memory_space=pltpu.SMEM), rows, rows],
        out_specs=pl.BlockSpec((TAPS, block, outputs), lambda i: (0, i, 0)),
        out_shape=jax.ShapeDtypeStruct((TAPS, inputs, outputs), F32),
        compiler_params=pltpu.CompilerParams(vmem_limit_bytes=16 * 2**20),
        name="conv_unpack",
    )(side.astype(jnp.int32)[None], own, other)


def conv_chunk(at, kernel):
    halves = pack(kernel.reshape((TAPS,) + kernel.shape[2:]))
    other = swap_half(pick(halves, 1 - at.half, 0))
    return row_major(pair(pick(halves, at.half, 0), other, at.half, 0))


def conv_weights_back(at, grad, inputs):
    total = image_total(at, grad.reshape(at.images, 2 * inputs, -1))
    other = swap_half(part(total, 1 - at.half, 2).astype(BF16))
    grad = unpack(at.half, part(total, at.half, 2), other)
    return grad.reshape((3, 3) + grad.shape[1:])


def by_heads(x):
    return x.reshape(x.shape[0], -1, DH)


def attend(queries, blocks):
    q_heads = by_heads(queries)
    scores = [
        jnp.einsum("qhd,khd->hqk", q_heads, by_heads(keys), preferred_element_type=F32)
        * (1.0 / math.sqrt(DH))
        for keys, values in blocks
    ]
    peak = scores[0].max(axis=-1, keepdims=True)
    for one in scores[1:]:
        peak = jnp.maximum(peak, one.max(axis=-1, keepdims=True))
    raised = [jnp.exp(one - peak) for one in scores]
    total = sum(one.sum(axis=-1, keepdims=True) for one in raised)
    joined = sum(
        jnp.einsum(
            "hqk,khd->qhd",
            (one / total).astype(BF16),
            by_heads(values),
            preferred_element_type=F32,
        )
        for one, (keys, values) in zip(raised, blocks)
    )
    return joined.reshape(queries.shape).astype(BF16), peak + jnp.log(total)


def attend_back(grad_out, queries, blocks, log_total):
    scaling = 1.0 / math.sqrt(DH)
    q_heads, g_heads = by_heads(queries), by_heads(grad_out)
    probs, slopes = [], []
    for keys, values in blocks:
        scores = jnp.einsum("qhd,khd->hqk", q_heads, by_heads(keys), preferred_element_type=F32)
        probs.append(jnp.exp(scores * scaling - log_total))
        slopes.append(
            jnp.einsum("qhd,khd->hqk", g_heads, by_heads(values), preferred_element_type=F32)
        )
    center = sum(
        jnp.sum(one * slope, axis=-1, keepdims=True) for one, slope in zip(probs, slopes)
    )
    grad_query, grad_blocks = 0.0, []
    for one, slope, (keys, values) in zip(probs, slopes, blocks):
        grad_scores = (one * (slope - center)).astype(BF16)
        grad_query = grad_query + jnp.einsum(
            "hqk,khd->qhd", grad_scores, by_heads(keys), preferred_element_type=F32
        )
        grad_keys = scaling * jnp.einsum(
            "hqk,qhd->khd", grad_scores, q_heads, preferred_element_type=F32
        )
        grad_values = jnp.einsum(
            "hqk,qhd->khd", one.astype(BF16), g_heads, preferred_element_type=F32
        )
        grad_blocks.append(
            jnp.concatenate(
                [grad_keys.reshape(keys.shape), grad_values.reshape(values.shape)], axis=1
            )
        )
    return (grad_query * scaling).reshape(queries.shape).astype(BF16), grad_blocks


def on_device(
    latents,
    text,
    step_count,
    time_index,
    conv1_w,
    conv2_w,
    time_w,
    proj_in_w,
    qkv_w,
    self_out_w,
    cross_q_w,
    cross_kv_w,
    cross_out_w,
    ff_in_w,
    ff_out_w,
    proj_out_w,
    gn_params,
    ln_params,
    biases,
    ff_bias,
    cotangent,
):
    at = Place()
    columns = latents.shape[2]
    width = latents.shape[3]
    tokens = latents.shape[1] * columns
    half = width // 2
    inputs = time_w.shape[0]
    hidden = ff_in_w.shape[2]

    own_params = jnp.concatenate([ln_params.reshape(6, width), biases[4:7]], axis=0)
    wide = pair(own_params, swap_core(own_params), at.core, 1)
    wide = pair(wide, swap_far(wide), at.far, 1)
    ln_wide, bias_self, bias_cross, bias_narrow = wide[:6].reshape(3, 2, C), wide[6], wide[7], wide[8]
    gn_own = part(gn_params, at.half, 2, 2)
    bias_own = part(biases, at.half, 2, 1)

    images = step_count.shape[0]
    moment = (999 - 1000 * time_index // step_count).astype(F32)
    half_width = C // 2
    channel = at.row * inputs + jnp.arange(inputs)
    frequency = jnp.exp(-math.log(10000.0) * (channel % half_width).astype(F32) / half_width)
    angles = moment[:, None] * frequency[None, :]
    embedding = jnp.where(channel[None, :] < half_width, jnp.cos(angles), jnp.sin(angles))
    temb_low = jax.nn.silu(embedding).astype(BF16)
    shift_all = rows_total(jnp.dot(temb_low, time_w, preferred_element_type=F32))
    shift_time = lax.dynamic_index_in_dim(shift_all, at.image, 0, keepdims=False)
    shift_time = part(shift_time, at.half, 2) + bias_own[1]

    text_own = part(text, at.row, lax.axis_size("rows"), 2)
    pair_w = cross_kv_w.reshape(cross_kv_w.shape[0], -1)
    kv_part = jnp.einsum("isc,cd->isd", text_own, pair_w, preferred_element_type=F32)
    kv_image = small_scatter(at, kv_part.astype(BF16))

    source = to_image(at, latents.reshape(tokens, width).T).astype(F32)
    norm_one, stored_one = group_forward(source, gn_own[0, 0], gn_own[0, 1], EPS_RES)

    chunk_one = conv_chunk(at, conv1_w)
    chunk_two = conv_chunk(at, conv2_w)
    square = jnp.concatenate(
        [
            qkv_w[:, 1],
            qkv_w[:, 2],
            qkv_w[:, 0],
            proj_in_w,
            self_out_w.T,
            cross_q_w,
            cross_out_w.T,
            proj_out_w,
        ],
        axis=1,
    )
    wide = jnp.concatenate([ff_in_w[:, 0], ff_in_w[:, 1], ff_out_w.T], axis=1)
    cross_kv = (kv_image + swap_half(kv_image.astype(BF16)).astype(F32)).astype(BF16)
    cross_keys, cross_values = cross_kv[:, :width], cross_kv[:, width:]
    conv_one = row_major(image_spread(at, chunk_one))
    conv_two = row_major(image_spread(at, chunk_two))
    low_one = jax.nn.silu(norm_one).astype(BF16)
    w_square = rows_gather(square)
    w_kvq, w_rest = w_square[:, : 3 * width], w_square[:, 3 * width :]
    w_in, w_self, w_query, w_cross, w_out = (
        w_rest[:, i * width : (i + 1) * width] for i in range(5)
    )
    w_wide = rows_gather(wide)
    w_value, w_gate, w_narrow = (w_wide[:, i * hidden : (i + 1) * hidden] for i in range(3))

    cot_rows = cotangent.reshape(tokens, width)
    cot_image = to_image(at, cot_rows.T).astype(F32)
    act_one = plane_gather(at, low_one)
    hidden_two = conv_forward(conv_one, act_one, columns)
    hidden_two = hidden_two + (bias_own[0] + shift_time)[:, None]
    norm_two, stored_two = group_forward(hidden_two, gn_own[1, 0], gn_own[1, 1], EPS_RES)
    act_two = plane_gather(at, jax.nn.silu(norm_two).astype(BF16))
    resid = source + conv_forward(conv_two, act_two, columns) + bias_own[2][:, None]
    norm_three, stored_three = group_forward(resid, gn_own[2, 0], gn_own[2, 1], EPS_MID)
    gin = channel_rows_gather(at, from_image(at, norm_three.astype(BF16)))
    resid_own = from_image(at, resid)

    stream_zero = to_tokens(at, dot(gin, w_in, 0, 0) + biases[3])
    ln_low_one, stored_ln_one = layer_forward(stream_zero, ln_wide[0])
    n_one = heads_gather(at, ln_low_one)
    kv_own = dot(n_one, w_kvq[:, : 2 * width], 1, 0, BF16)
    kv_other = swap_half(kv_own)
    queries = dot(n_one, w_kvq[:, 2 * width :], 1, 0, BF16)
    self_blocks = [(kv[:, :width], kv[:, width:]) for kv in (kv_own, kv_other)]
    attended, log_self = attend(queries, self_blocks)
    stream_one = stream_zero + heads_scatter(at, dot(attended, w_self, 1, 1, BF16)) + bias_self

    low_two, stored_ln_two = layer_forward(stream_one, ln_wide[1])
    n_two = heads_gather(at, low_two)
    cross_query = dot(n_two, w_query, 1, 0, BF16)
    cross_blocks = [(cross_keys, cross_values)]
    cross_att, log_cross = attend(cross_query, cross_blocks)
    stream_two = stream_one + heads_scatter(at, dot(cross_att, w_cross, 1, 1, BF16)) + bias_cross

    low_three, stored_ln_three = layer_forward(stream_two, ln_wide[2])
    n_three = heads_gather(at, low_three)
    value_in = dot(n_three, w_value, 1, 0) + ff_bias[0]
    gate_in = dot(n_three, w_gate, 1, 0) + ff_bias[1]
    cdf = 0.5 * (1.0 + lax.erf(gate_in / math.sqrt(2.0)))
    gelu = gate_in * cdf
    mixed = (value_in * gelu).astype(BF16)
    stream_three = stream_two + heads_scatter(at, dot(mixed, w_narrow, 1, 1, BF16)) + bias_narrow
    three = heads_gather(at, stream_three.astype(BF16))
    result = resid_own + (dot(w_out, three, 0, 1) + biases[7][:, None])
    output = result.astype(BF16).T.reshape(latents.shape)

    out_grad = dot(three, cot_rows, 0, 0, BF16)
    bias_seven = jnp.sum(cot_rows.astype(F32), axis=0)
    grad_three = heads_scatter(at, dot(cot_rows, w_out, 1, 1, BF16))
    low_ff = grad_three.astype(BF16)
    grad_ff = heads_gather(at, low_ff)
    narrow_grad = row_major(dot(grad_ff, mixed, 0, 0, BF16))
    grad_mixed = dot(grad_ff, w_narrow, 1, 0, BF16).astype(F32)
    pdf = jnp.exp(-0.5 * gate_in * gate_in) / math.sqrt(2.0 * math.pi)
    grad_value = (grad_mixed * gelu).astype(BF16)
    grad_gate = (grad_mixed * value_in * (cdf + gate_in * pdf)).astype(BF16)
    ffbias_grad = jnp.stack(
        [jnp.sum(grad_value.astype(F32), axis=0), jnp.sum(grad_gate.astype(F32), axis=0)]
    )
    grad_ln = heads_scatter(
        at, (dot(grad_value, w_value, 1, 1) + dot(grad_gate, w_gate, 1, 1)).astype(BF16)
    )
    wide_grad = row_major(
        dot(n_three, jnp.concatenate([grad_value, grad_gate], axis=1), 0, 0, BF16)
    )
    back, ln_grad_three = layer_backward(grad_ln, ln_wide[2], stored_ln_three)
    grad_two = grad_three + back

    low_cross = grad_two.astype(BF16)
    grad_cross = heads_gather(at, low_cross)
    cross_grad = dot(grad_cross, cross_att, 0, 0, BF16)
    grad_cross_att = dot(grad_cross, w_cross, 1, 0, BF16)
    grad_cq, (grad_ckv,) = attend_back(grad_cross_att, cross_query, cross_blocks, log_cross)
    query_grad = dot(n_two, grad_cq, 0, 0, BF16)
    grad_ckv = (grad_ckv + swap_half(grad_ckv.astype(BF16)).astype(F32)).astype(BF16)
    grad_ckv = small_gather(at, grad_ckv)
    pair_grad = jnp.einsum("isc,isd->cd", text_own, grad_ckv, preferred_element_type=F32)
    grad_ln = heads_scatter(at, dot(grad_cq, w_query, 1, 1, BF16))
    back, ln_grad_two = layer_backward(grad_ln, ln_wide[1], stored_ln_two)
    grad_one = grad_two + back

    low_self = grad_one.astype(BF16)
    grad_self = heads_gather(at, low_self)
    self_grad = dot(grad_self, attended, 0, 0, BF16)
    grad_attended = dot(grad_self, w_self, 1, 0, BF16)
    grad_q, (grad_kv, grad_kv_other) = attend_back(grad_attended, queries, self_blocks, log_self)
    grad_kv = (grad_kv + swap_half(grad_kv_other.astype(BF16)).astype(F32)).astype(BF16)
    grad_kvq = jnp.concatenate([grad_kv, grad_q], axis=1)
    kvq_grad = dot(n_one, grad_kvq, 0, 0, BF16)
    grad_ln = heads_scatter(at, dot(grad_kvq, w_kvq, 1, 1, BF16))
    back, ln_grad_one = layer_backward(grad_ln, ln_wide[0], stored_ln_one)
    grad_zero = to_channels(at, (grad_one + back).astype(BF16))
    in_grad = dot(gin, grad_zero, 1, 0, BF16)
    bias_three = jnp.sum(grad_zero.astype(F32), axis=0)
    grad_gin = channel_rows_scatter(at, dot(w_in, grad_zero, 1, 1, BF16))

    own_half = pick(grad_gin.reshape(2, half, tokens), at.half, 0)
    other_half = pick(grad_gin.reshape(2, half, tokens), 1 - at.half, 0)
    grad_gin = pair(own_half, swap_half(other_half.astype(BF16)).astype(F32), at.half, 1)
    back, gn_grad_three = group_backward(grad_gin, gn_own[2, 0], stored_three)
    grad_resid = cot_image + back
    grad_c_two = grad_resid.astype(BF16)
    bias_two = jnp.sum(grad_c_two.astype(F32), axis=1)
    spread_two = tap_spread(grad_c_two, columns)
    grad_act = plane_scatter(at, dot(conv_two, spread_two, 1, 0, BF16))
    conv_two_grad = row_major(dot(act_two, spread_two, 1, 1, BF16))
    grad_hidden, gn_grad_two = group_backward(
        grad_act * silu_slope(norm_two), gn_own[1, 0], stored_two
    )
    image_sum = jnp.sum(grad_hidden, axis=1)
    grad_c_one = grad_hidden.astype(BF16)
    bias_zero = jnp.sum(grad_c_one.astype(F32), axis=1)
    spread_one = tap_spread(grad_c_one, columns)
    grad_act = plane_scatter(at, dot(conv_one, spread_one, 1, 0, BF16))
    conv_one_grad = row_major(dot(act_one, spread_one, 1, 1, BF16))
    back, gn_grad_one = group_backward(
        grad_act * silu_slope(norm_one), gn_own[0, 0], stored_one
    )
    latents_grad = from_image(at, grad_resid + back).T.reshape(latents.shape)

    narrow = rows_scatter(narrow_grad)
    wide_out = rows_scatter(wide_grad)
    value, gate = wide_out[:, :hidden], wide_out[:, hidden:]
    rest_out = rows_scatter(
        row_major(
            jnp.concatenate(
                [kvq_grad, in_grad, self_grad, query_grad, cross_grad, out_grad], axis=1
            )
        )
    )
    rest = [rest_out[:, i * width : (i + 1) * width] for i in range(8)]
    conv_two_out = conv_weights_back(at, conv_two_grad, inputs)
    conv_one_out = conv_weights_back(at, conv_one_grad, inputs)

    token_sums = jnp.stack(
        ln_grad_one
        + ln_grad_two
        + ln_grad_three
        + [jnp.sum(low.astype(F32), axis=0) for low in (low_self, low_cross, low_ff)]
    )
    wide_half = C // 2
    keep = jnp.where(at.far == 0, token_sums[:, :wide_half], token_sums[:, wide_half:])
    send = jnp.where(at.far == 0, token_sums[:, wide_half:], token_sums[:, :wide_half])
    keep = keep + swap_far(send)
    own = jnp.where(at.core == 0, keep[:, :width], keep[:, width:])
    send = jnp.where(at.core == 0, keep[:, width:], keep[:, :width])
    own = own + swap_core(send)
    own = jnp.concatenate(
        [own, bias_three[None], bias_seven[None], ffbias_grad.reshape(-1, width)], axis=0
    )
    own = rows_total(own)
    ln_total = own[:6].reshape(3, 2, width)
    ffbias_total = own[11:].reshape(2, hidden)
    image_sums = jnp.stack(
        gn_grad_one + gn_grad_two + gn_grad_three + [bias_zero, image_sum, bias_two]
    )
    image_sums = image_stack(at, image_sums)
    image_sums = pair(image_sums, swap_half(image_sums), at.half, 2)
    totals = jnp.sum(image_sums, axis=0)
    gn_total = totals[:6].reshape(3, 2, width)
    bias_total = jnp.concatenate([totals[6:9], own[9:10], own[6:9], own[10:11]], axis=0)
    time_grad = lax.dot_general(
        temb_low.astype(F32),
        image_sums[:, 7],
        (((0,), (0,)), ((), ())),
        precision=lax.Precision.HIGHEST,
        preferred_element_type=F32,
    )

    return (
        output,
        latents_grad,
        conv_one_out,
        conv_two_out,
        time_grad,
        rest[3],
        jnp.stack([rest[2], rest[0], rest[1]], axis=1),
        rest[4].T,
        rest[5],
        pair_grad.reshape(cross_kv_w.shape),
        rest[6].T,
        jnp.stack([value, gate], axis=1),
        narrow.T,
        rest[7],
        gn_total,
        ln_total,
        bias_total,
        ffbias_total,
    )


def solution(mesh):
    return jax.shard_map(
        on_device,
        mesh=mesh,
        in_specs=(
            P("rows", None, None, "heads"),
            P(),
            P(),
            P(),
            P(None, None, "rows", "heads"),
            P(None, None, "rows", "heads"),
            P("rows", "heads"),
            P("rows", "heads"),
            P("rows", None, "heads"),
            P("heads", "rows"),
            P("rows", "heads"),
            P("rows", None, "heads"),
            P("heads", "rows"),
            P("rows", None, "heads"),
            P("heads", "rows"),
            P("rows", "heads"),
            P(None, None, "heads"),
            P(None, None, "heads"),
            P(None, "heads"),
            P(None, "heads"),
            P("rows", None, None, "heads"),
        ),
        out_specs=(
            P("rows", None, None, "heads"),
            P("rows", None, None, "heads"),
            P(None, None, "rows", "heads"),
            P(None, None, "rows", "heads"),
            P("rows", "heads"),
            P("rows", "heads"),
            P("rows", None, "heads"),
            P("heads", "rows"),
            P("rows", "heads"),
            P("rows", None, "heads"),
            P("heads", "rows"),
            P("rows", None, "heads"),
            P("heads", "rows"),
            P("rows", "heads"),
            P(None, None, "heads"),
            P(None, None, "heads"),
            P(None, "heads"),
            P(None, "heads"),
        ),
        check_vma=False,
    )
```

```python
import math

import jax
import jax.numpy as jnp
from jax import lax
from jax.experimental import pallas as pl
from jax.experimental.layout import Layout, with_layout_constraint
from jax.sharding import PartitionSpec as P
from jax.experimental.pallas import tpu as pltpu

C = 1280
DH = 64
GROUPS = 32
MEMBER = C // GROUPS
TAPS = 9
UNROLL = 8

EPS_RES = 1e-05
EPS_MID = 1e-06
EPS_LAYER = 1e-05

F32 = jnp.float32
BF16 = jnp.bfloat16


def dot(a, b, a_dim, b_dim, kind=F32):
    return lax.dot_general(
        a, b, (((a_dim,), (b_dim,)), ((), ())), preferred_element_type=F32
    ).astype(kind)


def row_major(x):
    return with_layout_constraint(x, Layout(tuple(range(x.ndim))))


def together(*values):
    return lax.optimization_barrier(values)


def swap(x, axis, mask):
    return lax.ppermute(x, axis, [(i, i ^ mask) for i in range(lax.axis_size(axis))])


def swap_half(x):
    return swap(x, "rows", 1)


def swap_core(x):
    return swap(x, "heads", 1)


def swap_far(x):
    return swap(x, "heads", 2)


def shift_image(x, images=1):
    n = lax.axis_size("rows")
    return lax.ppermute(x, "rows", [(i, (i + 2 * images) % n) for i in range(n)])


def pair(own, other, place, axis):
    return jnp.where(
        place == 0,
        jnp.concatenate([own, other], axis=axis),
        jnp.concatenate([other, own], axis=axis),
    )


def pick(x, place, axis):
    return lax.dynamic_index_in_dim(x, place, axis, keepdims=False)


def part(x, place, count, axis=0):
    size = x.shape[axis] // count
    return lax.dynamic_slice_in_dim(x, place * size, size, axis)


class Place:
    def __init__(self):
        row = lax.axis_index("rows")
        head = lax.axis_index("heads")
        self.row = row
        self.half = row % 2
        self.image = row // 2
        self.images = lax.axis_size("rows") // 2
        self.core = head % 2
        self.far = head // 2
        self.head = head


def image_gather(at, chunk):
    n, size = at.images, chunk.shape[0]
    whole = jnp.zeros((n * size,) + chunk.shape[1:], chunk.dtype)

    def put(whole, chunk, step):
        start = lax.rem(at.image - step + n, n) * size
        return lax.dynamic_update_slice_in_dim(whole, chunk, start, 0)

    if n > UNROLL:

        def body(step, carry):
            whole, chunk = carry
            return put(whole, chunk, step), shift_image(chunk)

        return lax.fori_loop(0, n, body, (whole, chunk))[0]
    for step in range(n):
        whole = put(whole, chunk, step)
        if step < n - 1:
            chunk = shift_image(chunk)
    return whole


def rows_gather(chunk):
    return lax.all_gather(chunk, "rows", axis=0, tiled=True)


def rows_scatter(grad):
    return lax.psum_scatter(grad, "rows", scatter_dimension=0, tiled=True).astype(F32)


def small_gather(at, x):
    n = at.images
    if n > UNROLL:
        return image_gather(at, x[None])
    whole = jnp.zeros((n,) + x.shape, x.dtype)
    for step in range(n):
        other = shift_image(x, step) if step else x
        start = lax.rem(at.image - step + n, n)
        whole = lax.dynamic_update_index_in_dim(whole, other, start, 0)
    return whole


def small_scatter(at, blocks):
    n = at.images
    if n > UNROLL:
        return image_scatter(at, blocks)
    total = lax.dynamic_index_in_dim(blocks, at.image, 0, keepdims=False).astype(F32)
    for step in range(1, n):
        block = lax.dynamic_index_in_dim(
            blocks, lax.rem(at.image + step, n), 0, keepdims=False
        )
        total = total + shift_image(block, step).astype(F32)
    return total


def image_scatter(at, blocks):
    n = at.images

    def local(step):
        return lax.dynamic_index_in_dim(
            blocks, lax.rem(at.image - 1 - step + 2 * n, n), 0, keepdims=False
        )

    def advance(step, moving):
        return shift_image(moving).astype(F32) + local(step + 1).astype(F32)

    moving = local(0)
    if n > UNROLL:
        moving = lax.fori_loop(
            0, n - 2, lambda step, value: advance(step, value).astype(blocks.dtype), moving
        )
    else:
        for step in range(n - 2):
            moving = advance(step, moving).astype(blocks.dtype)
    return advance(n - 2, moving)


def image_spread(at, chunk):
    if at.images != 4:
        return image_gather(at, chunk)
    size = chunk.shape[0]
    up, down = shift_image(chunk, 1), shift_image(chunk, 3)
    far = (shift_image(up[: size // 2], 1), shift_image(down[size // 2 :], 3))
    whole = jnp.concatenate([chunk] * 4, axis=0)
    for move, block in ((3, up), (1, down), (2, jnp.concatenate(far, axis=0))):
        start = lax.rem(at.image + move, 4) * size
        whole = lax.dynamic_update_slice_in_dim(whole, block, start, 0)
    return whole


def add_low(a, b):
    return (a.astype(F32) + b.astype(F32)).astype(BF16)


def image_total(at, blocks, gate=None):
    if at.images != 4:
        return image_scatter(at, blocks), gate

    def local(move):
        place = lax.rem(at.image + move, 4)
        return lax.dynamic_index_in_dim(blocks, place, 0, keepdims=False)

    size = blocks.shape[1] // 2
    far, up, down = local(2), local(1), local(3)
    first, second = shift_image(far[:size], 1), shift_image(far[size:], 3)
    if gate is not None:
        first, second, gate = together(first, second, gate)
    up = jnp.concatenate([add_low(up[:size], first), up[size:]], axis=0)
    down = jnp.concatenate([down[:size], add_low(down[size:], second)], axis=0)
    up, down = shift_image(up, 1), shift_image(down, 3)
    return local(0).astype(F32) + up.astype(F32) + down.astype(F32), gate


def rows_total(x, first=1):
    mask = first
    while mask < lax.axis_size("rows"):
        x = x + swap(x, "rows", mask)
        mask *= 2
    return x


def image_stack(at, x):
    x = x[None]
    mask = 1
    while mask < at.images:
        x = pair(x, swap(x, "rows", 2 * mask), (at.image // mask) % 2, 0)
        mask *= 2
    return x


def heads_scatter(at, grad):
    own = part(grad, at.core, 2).astype(F32)
    own = own + swap_core(part(grad, 1 - at.core, 2)).astype(F32)
    other = swap_far(part(own, 1 - at.far, 2).astype(BF16))
    return part(own, at.far, 2) + other.astype(F32)


def heads_gather(at, quarter):
    two = pair(quarter, swap_far(quarter), at.far, 0)
    return pair(two, swap_core(two), at.core, 0)


def to_tokens(at, x):
    other = swap_core(part(x, 1 - at.core, 2).astype(BF16)).astype(F32)
    x = pair(part(x, at.core, 2), other, at.core, 1)
    other = swap_far(part(x, 1 - at.far, 2).astype(BF16)).astype(F32)
    return pair(part(x, at.far, 2), other, at.far, 1)


def to_channels(at, x):
    wide = x.shape[1] // 2
    first, second = x[:, :wide], x[:, wide:]
    other = swap_far(jnp.where(at.far == 0, second, first))
    x = pair(jnp.where(at.far == 0, first, second), other, at.far, 0)
    wide = wide // 2
    first, second = x[:, :wide], x[:, wide:]
    other = swap_core(jnp.where(at.core == 0, second, first))
    return pair(jnp.where(at.core == 0, first, second), other, at.core, 0)


def channel_rows_gather(at, x):
    shape = x.shape
    x = pair(x[None], swap_far(x)[None], at.far, 0)
    x = pair(x[:, None], swap_core(x)[:, None], at.core, 1)
    return x.reshape((-1,) + shape[1:])


def channel_rows_scatter(at, x):
    blocks = x.reshape(2, 2, -1, x.shape[1])
    own = pick(blocks, at.core, 1).astype(F32)
    own = own + swap_core(pick(blocks, 1 - at.core, 1)).astype(F32)
    other = swap_far(pick(own, 1 - at.far, 0).astype(BF16))
    return pick(own, at.far, 0) + other.astype(F32)


def to_image(at, x):
    blocks = x.reshape(2, -1, x.shape[1])
    return pair(pick(blocks, at.half, 0), swap_half(pick(blocks, 1 - at.half, 0)), at.half, 1)


def from_image(at, x):
    return pair(
        part(x, at.half, 2, 1), swap_half(part(x, 1 - at.half, 2, 1)), at.half, 0
    )


def plane_gather(at, x):
    width, tokens = x.shape
    left, right = x[:, : tokens // 2], x[:, tokens // 2 :]
    left = pair(left[None], swap_half(left)[None], at.half, 0)
    right = pair(right[None], swap_far(right)[None], at.far, 0)
    left = pair(left[None], swap_far(left)[None], at.far, 0)
    right = pair(right[:, None], swap_half(right)[:, None], at.half, 1)
    x = jnp.concatenate([left, right], axis=3)
    x = pair(x[:, None], swap_core(x)[:, None], at.core, 1)
    return x.reshape(8 * width, tokens)


def plane_scatter(at, x):
    tokens = x.shape[1]
    blocks = x.reshape(2, 2, 2, -1, tokens)
    own = pick(blocks, at.core, 1).astype(F32)
    own = own + swap_core(pick(blocks, 1 - at.core, 1)).astype(F32)
    left, right = own[..., : tokens // 2], own[..., tokens // 2 :]
    left = pick(left, at.half, 1) + swap_half(pick(left, 1 - at.half, 1).astype(BF16)).astype(F32)
    right = pick(right, at.far, 0) + swap_far(pick(right, 1 - at.far, 0).astype(BF16)).astype(F32)
    left = pick(left, at.far, 0) + swap_far(pick(left, 1 - at.far, 0).astype(BF16)).astype(F32)
    right = pick(right, at.half, 0) + swap_half(pick(right, 1 - at.half, 0).astype(BF16)).astype(
        F32
    )
    return jnp.concatenate([left, right], axis=1)


def group_forward(inputs, gain, shift, epsilon):
    grouped = inputs.reshape(-1, MEMBER, inputs.shape[1])
    center = jnp.mean(grouped, axis=(1, 2), keepdims=True)
    inverse = lax.rsqrt(jnp.mean(jnp.square(grouped - center), axis=(1, 2), keepdims=True) + epsilon)
    normed = ((grouped - center) * inverse).reshape(inputs.shape)
    return normed * gain[:, None] + shift[:, None], (normed, inverse)


def group_backward(gradient, gain, stored):
    normed, inverse = stored
    shape = gradient.shape
    scaled = (gradient * gain[:, None]).reshape(-1, MEMBER, shape[1])
    flat = normed.reshape(scaled.shape)
    first = jnp.mean(scaled, axis=(1, 2), keepdims=True)
    second = jnp.mean(scaled * flat, axis=(1, 2), keepdims=True)
    back = (inverse * (scaled - first - flat * second)).reshape(shape)
    return back, [jnp.sum(gradient * normed, axis=1), jnp.sum(gradient, axis=1)]


def layer_forward(inputs, params):
    center = jnp.mean(inputs, axis=1, keepdims=True)
    inverse = lax.rsqrt(jnp.mean(jnp.square(inputs - center), axis=1, keepdims=True) + EPS_LAYER)
    normed = (inputs - center) * inverse
    return (normed * params[0] + params[1]).astype(BF16), (normed, inverse)


def layer_backward(gradient, params, stored):
    normed, inverse = stored
    scaled = gradient * params[0]
    first = jnp.mean(scaled, axis=1, keepdims=True)
    second = jnp.mean(scaled * normed, axis=1, keepdims=True)
    back = inverse * (scaled - first - normed * second)
    return back, [jnp.sum(gradient * normed, axis=0), jnp.sum(gradient, axis=0)]


def silu_slope(inputs):
    sigma = jax.nn.sigmoid(inputs)
    return sigma * (1.0 + inputs * (1.0 - sigma))


def tap_mask(shape, tap, columns):
    place = lax.broadcasted_iota(jnp.int32, shape, 1)
    line, column = place // columns, place % columns
    keep = None
    for value, step, count in (
        (line, tap // 3 - 1, shape[1] // columns),
        (column, tap % 3 - 1, columns),
    ):
        if step != 0:
            inside = value >= 1 if step < 0 else value <= count - 2
            keep = inside if keep is None else jnp.logical_and(keep, inside)
    return keep


def tap_offset(tap, columns):
    return (tap // 3 - 1) * columns + tap % 3 - 1


def conv_kernel(columns, weights_ref, acts_ref, sum_ref, taps_ref):
    width, tokens = sum_ref.shape
    acts = acts_ref[...]
    for start in range(0, TAPS * width, 256):
        cut = slice(start, min(start + 256, TAPS * width))
        taps_ref[cut, :] = lax.dot_general(
            weights_ref[:, cut], acts, (((0,), (0,)), ((), ())), preferred_element_type=F32
        )
    for start in range(0, width, 32):
        total = taps_ref[4 * width + start : 4 * width + start + 32, :]
        for tap in range(TAPS):
            if tap != 4:
                taps = taps_ref[tap * width + start : tap * width + start + 32, :]
                moved = pltpu.roll(taps, -tap_offset(tap, columns) % tokens, 1)
                total = total + jnp.where(tap_mask(moved.shape, tap, columns), moved, 0.0)
        sum_ref[start : start + 32, :] = total


def conv_forward(weights, acts, columns):
    tokens = acts.shape[1]
    width = weights.shape[1] // TAPS
    return pl.pallas_call(
        lambda *refs: conv_kernel(columns, *refs),
        in_specs=[pl.BlockSpec(memory_space=pltpu.VMEM)] * 2,
        out_specs=pl.BlockSpec(memory_space=pltpu.VMEM),
        out_shape=jax.ShapeDtypeStruct((width, tokens), F32),
        scratch_shapes=[pltpu.VMEM((TAPS * width, tokens), F32)],
        compiler_params=pltpu.CompilerParams(vmem_limit_bytes=40 * 2**20),
        cost_estimate=pl.CostEstimate(
            flops=2 * weights.size * tokens, bytes_accessed=2 * weights.size, transcendentals=0
        ),
        name="conv_forward",
    )(weights, acts)


def tap_spread_kernel(columns, grad_ref, taps_ref):
    tokens = grad_ref.shape[1]
    grad = grad_ref[...].astype(F32)
    for tap in range(TAPS):
        if tap == 4:
            taps_ref[tap] = grad_ref[...]
            continue
        moved = pltpu.roll(grad, tap_offset(tap, columns) % tokens, 1)
        keep = tap_mask(moved.shape, TAPS - 1 - tap, columns)
        taps_ref[tap] = jnp.where(keep, moved, 0.0).astype(taps_ref.dtype)


def tap_spread(grad, columns):
    width, tokens = grad.shape
    block = 32
    return pl.pallas_call(
        lambda *refs: tap_spread_kernel(columns, *refs),
        grid=(width // block,),
        in_specs=[pl.BlockSpec((block, tokens), lambda i: (i, 0))],
        out_specs=pl.BlockSpec((TAPS, block, tokens), lambda i: (0, i, 0)),
        out_shape=jax.ShapeDtypeStruct((TAPS, width, tokens), BF16),
        compiler_params=pltpu.CompilerParams(vmem_limit_bytes=16 * 2**20),
        name="tap_spread",
    )(grad).reshape(TAPS * width, tokens)


def pack_kernel(kernel_ref, halves_ref):
    half = kernel_ref.shape[2] // 2
    taps = [kernel_ref[tap].astype(F32) for tap in range(TAPS)]
    for side in range(2):
        row = jnp.concatenate([tap[:, side * half : (side + 1) * half] for tap in taps], axis=1)
        halves_ref[side] = row.astype(halves_ref.dtype)


def pack(kernel):
    taps, inputs, outputs = kernel.shape
    block = 32 if inputs % 32 == 0 else inputs
    return pl.pallas_call(
        pack_kernel,
        grid=(inputs // block,),
        in_specs=[pl.BlockSpec((taps, block, outputs), lambda i: (0, i, 0))],
        out_specs=pl.BlockSpec((2, block, taps * outputs // 2), lambda i: (0, i, 0)),
        out_shape=jax.ShapeDtypeStruct((2, inputs, taps * outputs // 2), kernel.dtype),
        compiler_params=pltpu.CompilerParams(vmem_limit_bytes=16 * 2**20),
        name="conv_pack",
    )(kernel)


def unpack_kernel(side_ref, own_ref, other_ref, kernel_ref):
    half = kernel_ref.shape[2] // 2
    first = side_ref[0] == 0
    own, other = own_ref[...], other_ref[...].astype(F32)
    low, high = jnp.where(first, own, other), jnp.where(first, other, own)
    for tap in range(TAPS):
        cut = slice(tap * half, (tap + 1) * half)
        kernel_ref[tap] = jnp.concatenate([low[:, cut], high[:, cut]], axis=1)


def unpack(side, own, other):
    inputs, width = own.shape
    outputs = 2 * width // TAPS
    block = 32 if inputs % 32 == 0 else inputs
    rows = pl.BlockSpec((block, width), lambda i: (i, 0))
    return pl.pallas_call(
        unpack_kernel,
        grid=(inputs // block,),
        in_specs=[pl.BlockSpec(memory_space=pltpu.SMEM), rows, rows],
        out_specs=pl.BlockSpec((TAPS, block, outputs), lambda i: (0, i, 0)),
        out_shape=jax.ShapeDtypeStruct((TAPS, inputs, outputs), F32),
        compiler_params=pltpu.CompilerParams(vmem_limit_bytes=16 * 2**20),
        name="conv_unpack",
    )(side.astype(jnp.int32)[None], own, other)


def conv_chunk(at, kernel):
    halves = pack(kernel.reshape((TAPS,) + kernel.shape[2:]))
    other = swap_half(pick(halves, 1 - at.half, 0))
    return row_major(pair(pick(halves, at.half, 0), other, at.half, 0))


def conv_weights_back(at, total):
    other = swap_half(part(total, 1 - at.half, 2).astype(BF16))
    grad = unpack(at.half, part(total, at.half, 2), other)
    return grad.reshape((3, 3) + grad.shape[1:])


def by_heads(x):
    return x.reshape(x.shape[0], -1, DH)


def attend(queries, blocks):
    q_heads = by_heads(queries)
    scores = [
        jnp.einsum("qhd,khd->hqk", q_heads, by_heads(keys), preferred_element_type=F32)
        * (1.0 / math.sqrt(DH))
        for keys, values in blocks
    ]
    peak = scores[0].max(axis=-1, keepdims=True)
    for one in scores[1:]:
        peak = jnp.maximum(peak, one.max(axis=-1, keepdims=True))
    raised = [jnp.exp(one - peak) for one in scores]
    total = sum(one.sum(axis=-1, keepdims=True) for one in raised)
    joined = sum(
        jnp.einsum(
            "hqk,khd->qhd",
            (one / total).astype(BF16),
            by_heads(values),
            preferred_element_type=F32,
        )
        for one, (keys, values) in zip(raised, blocks)
    )
    return joined.reshape(queries.shape).astype(BF16), peak + jnp.log(total)


def attend_back(grad_out, queries, blocks, log_total):
    scaling = 1.0 / math.sqrt(DH)
    q_heads, g_heads = by_heads(queries), by_heads(grad_out)
    probs, slopes = [], []
    for keys, values in blocks:
        scores = jnp.einsum("qhd,khd->hqk", q_heads, by_heads(keys), preferred_element_type=F32)
        probs.append(jnp.exp(scores * scaling - log_total))
        slopes.append(
            jnp.einsum("qhd,khd->hqk", g_heads, by_heads(values), preferred_element_type=F32)
        )
    center = sum(
        jnp.sum(one * slope, axis=-1, keepdims=True) for one, slope in zip(probs, slopes)
    )
    grad_query, grad_blocks = 0.0, []
    for one, slope, (keys, values) in zip(probs, slopes, blocks):
        grad_scores = (one * (slope - center)).astype(BF16)
        grad_query = grad_query + jnp.einsum(
            "hqk,khd->qhd", grad_scores, by_heads(keys), preferred_element_type=F32
        )
        grad_keys = scaling * jnp.einsum(
            "hqk,qhd->khd", grad_scores, q_heads, preferred_element_type=F32
        )
        grad_values = jnp.einsum(
            "hqk,qhd->khd", one.astype(BF16), g_heads, preferred_element_type=F32
        )
        grad_blocks.append(
            jnp.concatenate(
                [grad_keys.reshape(keys.shape), grad_values.reshape(values.shape)], axis=1
            )
        )
    return (grad_query * scaling).reshape(queries.shape).astype(BF16), grad_blocks


def on_device(
    latents,
    text,
    step_count,
    time_index,
    conv1_w,
    conv2_w,
    time_w,
    proj_in_w,
    qkv_w,
    self_out_w,
    cross_q_w,
    cross_kv_w,
    cross_out_w,
    ff_in_w,
    ff_out_w,
    proj_out_w,
    gn_params,
    ln_params,
    biases,
    ff_bias,
    cotangent,
):
    at = Place()
    columns = latents.shape[2]
    width = latents.shape[3]
    tokens = latents.shape[1] * columns
    half = width // 2
    inputs = time_w.shape[0]
    hidden = ff_in_w.shape[2]

    own_params = jnp.concatenate([ln_params.reshape(6, width), biases[4:7]], axis=0)
    wide = pair(own_params, swap_core(own_params), at.core, 1)
    wide = pair(wide, swap_far(wide), at.far, 1)
    ln_wide, bias_self, bias_cross, bias_narrow = wide[:6].reshape(3, 2, C), wide[6], wide[7], wide[8]
    gn_own = part(gn_params, at.half, 2, 2)
    bias_own = part(biases, at.half, 2, 1)

    images = step_count.shape[0]
    moment = (999 - 1000 * time_index // step_count).astype(F32)
    half_width = C // 2
    channel = at.row * inputs + jnp.arange(inputs)
    frequency = jnp.exp(-math.log(10000.0) * (channel % half_width).astype(F32) / half_width)
    angles = moment[:, None] * frequency[None, :]
    embedding = jnp.where(channel[None, :] < half_width, jnp.cos(angles), jnp.sin(angles))
    temb_low = jax.nn.silu(embedding).astype(BF16)
    shift_all = rows_total(jnp.dot(temb_low, time_w, preferred_element_type=F32))
    shift_time = lax.dynamic_index_in_dim(shift_all, at.image, 0, keepdims=False)
    shift_time = part(shift_time, at.half, 2) + bias_own[1]

    text_own = part(text, at.row, lax.axis_size("rows"), 2)
    pair_w = cross_kv_w.reshape(cross_kv_w.shape[0], -1)
    kv_part = jnp.einsum("isc,cd->isd", text_own, pair_w, preferred_element_type=F32)
    kv_image = small_scatter(at, kv_part.astype(BF16))

    source = to_image(at, latents.reshape(tokens, width).T).astype(F32)
    norm_one, stored_one = group_forward(source, gn_own[0, 0], gn_own[0, 1], EPS_RES)

    chunk_one = conv_chunk(at, conv1_w)
    chunk_two = conv_chunk(at, conv2_w)
    square = jnp.concatenate(
        [
            qkv_w[:, 1],
            qkv_w[:, 2],
            qkv_w[:, 0],
            proj_in_w,
            self_out_w.T,
            cross_q_w,
            cross_out_w.T,
            proj_out_w,
        ],
        axis=1,
    )
    wide = jnp.concatenate([ff_in_w[:, 0], ff_in_w[:, 1], ff_out_w.T], axis=1)
    cross_kv = (kv_image + swap_half(kv_image.astype(BF16)).astype(F32)).astype(BF16)
    cross_keys, cross_values = cross_kv[:, :width], cross_kv[:, width:]
    conv_two = row_major(image_spread(at, chunk_two))
    low_one = jax.nn.silu(norm_one).astype(BF16)
    w_square = rows_gather(square)
    w_kvq, w_rest = w_square[:, : 3 * width], w_square[:, 3 * width :]
    w_in, w_self, w_query, w_cross, w_out = (
        w_rest[:, i * width : (i + 1) * width] for i in range(5)
    )
    w_wide = rows_gather(wide)
    w_value, w_gate, w_narrow = (w_wide[:, i * hidden : (i + 1) * hidden] for i in range(3))

    cot_rows = cotangent.reshape(tokens, width)
    cot_image = to_image(at, cot_rows.T).astype(F32)
    low_one, chunk_one = together(low_one, chunk_one)
    conv_one = row_major(image_spread(at, chunk_one))
    act_one = plane_gather(at, low_one)
    hidden_two = conv_forward(conv_one, act_one, columns)
    hidden_two = hidden_two + (bias_own[0] + shift_time)[:, None]
    norm_two, stored_two = group_forward(hidden_two, gn_own[1, 0], gn_own[1, 1], EPS_RES)
    act_two = plane_gather(at, jax.nn.silu(norm_two).astype(BF16))
    resid = source + conv_forward(conv_two, act_two, columns) + bias_own[2][:, None]
    norm_three, stored_three = group_forward(resid, gn_own[2, 0], gn_own[2, 1], EPS_MID)
    gin = channel_rows_gather(at, from_image(at, norm_three.astype(BF16)))
    resid_own = from_image(at, resid)

    stream_zero = to_tokens(at, dot(gin, w_in, 0, 0) + biases[3])
    ln_low_one, stored_ln_one = layer_forward(stream_zero, ln_wide[0])
    n_one_x = heads_gather(at, ln_low_one)
    n_one, resid_own, cross_keys, cross_values = together(n_one_x, resid_own, cross_keys, cross_values)
    keys, values, queries = (
        dot(n_one, w_kvq[:, i * width : (i + 1) * width], 1, 0, BF16) for i in range(3)
    )
    self_blocks = [(keys, values), (swap_half(keys), swap_half(values))]
    attended, log_self = attend(queries, self_blocks)
    stream_one = stream_zero + heads_scatter(at, dot(attended, w_self, 1, 1, BF16)) + bias_self

    low_two, stored_ln_two = layer_forward(stream_one, ln_wide[1])
    n_two = heads_gather(at, low_two)
    cross_query = dot(n_two, w_query, 1, 0, BF16)
    cross_blocks = [(cross_keys, cross_values)]
    cross_att, log_cross = attend(cross_query, cross_blocks)
    stream_two = stream_one + heads_scatter(at, dot(cross_att, w_cross, 1, 1, BF16)) + bias_cross

    low_three, stored_ln_three = layer_forward(stream_two, ln_wide[2])
    n_three = heads_gather(at, low_three)
    value_in = dot(n_three, w_value, 1, 0) + ff_bias[0]
    gate_in = dot(n_three, w_gate, 1, 0) + ff_bias[1]
    cdf = 0.5 * (1.0 + lax.erf(gate_in / math.sqrt(2.0)))
    gelu = gate_in * cdf
    mixed = (value_in * gelu).astype(BF16)
    stream_three = stream_two + heads_scatter(at, dot(mixed, w_narrow, 1, 1, BF16)) + bias_narrow
    three = heads_gather(at, stream_three.astype(BF16))
    result = resid_own + (dot(w_out, three, 0, 1) + biases[7][:, None])
    output = result.astype(BF16).T.reshape(latents.shape)

    out_grad = dot(three, cot_rows, 0, 0, BF16)
    bias_seven = jnp.sum(cot_rows.astype(F32), axis=0)
    grad_three = heads_scatter(at, dot(cot_rows, w_out, 1, 1, BF16))
    low_ff = grad_three.astype(BF16)
    grad_ff = heads_gather(at, low_ff)
    narrow_grad = row_major(dot(grad_ff, mixed, 0, 0, BF16))
    grad_mixed = dot(grad_ff, w_narrow, 1, 0, BF16).astype(F32)
    pdf = jnp.exp(-0.5 * gate_in * gate_in) / math.sqrt(2.0 * math.pi)
    grad_value = (grad_mixed * gelu).astype(BF16)
    grad_gate = (grad_mixed * value_in * (cdf + gate_in * pdf)).astype(BF16)
    ffbias_grad = jnp.stack(
        [jnp.sum(grad_value.astype(F32), axis=0), jnp.sum(grad_gate.astype(F32), axis=0)]
    )
    grad_ln = heads_scatter(
        at, (dot(grad_value, w_value, 1, 1) + dot(grad_gate, w_gate, 1, 1)).astype(BF16)
    )
    wide_grad = row_major(
        dot(n_three, jnp.concatenate([grad_value, grad_gate], axis=1), 0, 0, BF16)
    )
    back, ln_grad_three = layer_backward(grad_ln, ln_wide[2], stored_ln_three)
    grad_two = grad_three + back

    low_cross = grad_two.astype(BF16)
    grad_cross = heads_gather(at, low_cross)
    cross_grad = dot(grad_cross, cross_att, 0, 0, BF16)
    grad_cross_att = dot(grad_cross, w_cross, 1, 0, BF16)
    grad_cq, (grad_ckv,) = attend_back(grad_cross_att, cross_query, cross_blocks, log_cross)
    query_grad = dot(n_two, grad_cq, 0, 0, BF16)
    grad_ckv = (grad_ckv + swap_half(grad_ckv.astype(BF16)).astype(F32)).astype(BF16)
    grad_ckv = small_gather(at, grad_ckv)
    pair_grad = jnp.einsum("isc,isd->cd", text_own, grad_ckv, preferred_element_type=F32)
    grad_ln = heads_scatter(at, dot(grad_cq, w_query, 1, 1, BF16))
    back, ln_grad_two = layer_backward(grad_ln, ln_wide[1], stored_ln_two)
    grad_one = grad_two + back

    low_self = grad_one.astype(BF16)
    grad_self = heads_gather(at, low_self)
    self_grad = dot(grad_self, attended, 0, 0, BF16)
    grad_attended = dot(grad_self, w_self, 1, 0, BF16)
    grad_q, (grad_kv, grad_kv_other) = attend_back(grad_attended, queries, self_blocks, log_self)
    grad_kv = (grad_kv + swap_half(grad_kv_other.astype(BF16)).astype(F32)).astype(BF16)
    grad_kvq = jnp.concatenate([grad_kv, grad_q], axis=1)
    kvq_grad = dot(n_one, grad_kvq, 0, 0, BF16)
    grad_ln = heads_scatter(at, dot(grad_kvq, w_kvq, 1, 1, BF16))
    back, ln_grad_one = layer_backward(grad_ln, ln_wide[0], stored_ln_one)
    grad_zero = to_channels(at, (grad_one + back).astype(BF16))
    in_grad = dot(gin, grad_zero, 1, 0, BF16)
    bias_three = jnp.sum(grad_zero.astype(F32), axis=0)
    grad_gin = channel_rows_scatter(at, dot(w_in, grad_zero, 1, 1, BF16))

    own_half = pick(grad_gin.reshape(2, half, tokens), at.half, 0)
    other_half = pick(grad_gin.reshape(2, half, tokens), 1 - at.half, 0)
    grad_gin = pair(own_half, swap_half(other_half.astype(BF16)).astype(F32), at.half, 1)
    back, gn_grad_three = group_backward(grad_gin, gn_own[2, 0], stored_three)
    grad_resid = cot_image + back
    grad_c_two = grad_resid.astype(BF16)
    bias_two = jnp.sum(grad_c_two.astype(F32), axis=1)
    spread_two = tap_spread(grad_c_two, columns)
    grad_act = plane_scatter(at, dot(conv_two, spread_two, 1, 0, BF16))
    conv_two_grad = row_major(dot(act_two, spread_two, 1, 1, BF16))
    total_two, grad_act = image_total(at, conv_two_grad.reshape(at.images, 2 * inputs, -1), grad_act)
    grad_hidden, gn_grad_two = group_backward(
        grad_act * silu_slope(norm_two), gn_own[1, 0], stored_two
    )
    image_sum = jnp.sum(grad_hidden, axis=1)
    grad_c_one = grad_hidden.astype(BF16)
    bias_zero = jnp.sum(grad_c_one.astype(F32), axis=1)
    spread_one = tap_spread(grad_c_one, columns)
    grad_act = plane_scatter(at, dot(conv_one, spread_one, 1, 0, BF16))
    conv_one_grad = row_major(dot(act_one, spread_one, 1, 1, BF16))
    total_one, grad_act = image_total(at, conv_one_grad.reshape(at.images, 2 * inputs, -1), grad_act)
    back, gn_grad_one = group_backward(
        grad_act * silu_slope(norm_one), gn_own[0, 0], stored_one
    )
    latents_grad = from_image(at, grad_resid + back).T.reshape(latents.shape)

    narrow = rows_scatter(narrow_grad)
    wide_out = rows_scatter(wide_grad)
    value, gate = wide_out[:, :hidden], wide_out[:, hidden:]
    rest_out = rows_scatter(
        row_major(
            jnp.concatenate(
                [kvq_grad, in_grad, self_grad, query_grad, cross_grad, out_grad], axis=1
            )
        )
    )
    rest = [rest_out[:, i * width : (i + 1) * width] for i in range(8)]
    conv_two_out = conv_weights_back(at, total_two)
    conv_one_out = conv_weights_back(at, total_one)

    token_sums = jnp.stack(
        ln_grad_one
        + ln_grad_two
        + ln_grad_three
        + [jnp.sum(low.astype(F32), axis=0) for low in (low_self, low_cross, low_ff)]
    )
    wide_half = C // 2
    keep = jnp.where(at.far == 0, token_sums[:, :wide_half], token_sums[:, wide_half:])
    send = jnp.where(at.far == 0, token_sums[:, wide_half:], token_sums[:, :wide_half])
    keep = keep + swap_far(send)
    own = jnp.where(at.core == 0, keep[:, :width], keep[:, width:])
    send = jnp.where(at.core == 0, keep[:, width:], keep[:, :width])
    own = own + swap_core(send)
    own = jnp.concatenate(
        [own, bias_three[None], bias_seven[None], ffbias_grad.reshape(-1, width)], axis=0
    )
    own = rows_total(own)
    ln_total = own[:6].reshape(3, 2, width)
    ffbias_total = own[11:].reshape(2, hidden)
    image_sums = jnp.stack(
        gn_grad_one + gn_grad_two + gn_grad_three + [bias_zero, image_sum, bias_two]
    )
    image_sums = image_stack(at, image_sums)
    image_sums = pair(image_sums, swap_half(image_sums), at.half, 2)
    totals = jnp.sum(image_sums, axis=0)
    gn_total = totals[:6].reshape(3, 2, width)
    bias_total = jnp.concatenate([totals[6:9], own[9:10], own[6:9], own[10:11]], axis=0)
    time_grad = lax.dot_general(
        temb_low.astype(F32),
        image_sums[:, 7],
        (((0,), (0,)), ((), ())),
        precision=lax.Precision.HIGHEST,
        preferred_element_type=F32,
    )

    return (
        output,
        latents_grad,
        conv_one_out,
        conv_two_out,
        time_grad,
        rest[3],
        jnp.stack([rest[2], rest[0], rest[1]], axis=1),
        rest[4].T,
        rest[5],
        pair_grad.reshape(cross_kv_w.shape),
        rest[6].T,
        jnp.stack([value, gate], axis=1),
        narrow.T,
        rest[7],
        gn_total,
        ln_total,
        bias_total,
        ffbias_total,
    )


def solution(mesh):
    return jax.shard_map(
        on_device,
        mesh=mesh,
        in_specs=(
            P("rows", None, None, "heads"),
            P(),
            P(),
            P(),
            P(None, None, "rows", "heads"),
            P(None, None, "rows", "heads"),
            P("rows", "heads"),
            P("rows", "heads"),
            P("rows", None, "heads"),
            P("heads", "rows"),
            P("rows", "heads"),
            P("rows", None, "heads"),
            P("heads", "rows"),
            P("rows", None, "heads"),
            P("heads", "rows"),
            P("rows", "heads"),
            P(None, None, "heads"),
            P(None, None, "heads"),
            P(None, "heads"),
            P(None, "heads"),
            P("rows", None, None, "heads"),
        ),
        out_specs=(
            P("rows", None, None, "heads"),
            P("rows", None, None, "heads"),
            P(None, None, "rows", "heads"),
            P(None, None, "rows", "heads"),
            P("rows", "heads"),
            P("rows", "heads"),
            P("rows", None, "heads"),
            P("heads", "rows"),
            P("rows", "heads"),
            P("rows", None, "heads"),
            P("heads", "rows"),
            P("rows", None, "heads"),
            P("heads", "rows"),
            P("rows", "heads"),
            P(None, None, "heads"),
            P(None, None, "heads"),
            P(None, "heads"),
            P(None, "heads"),
        ),
        check_vma=False,
    )
```
